32 devices in a mesh: section: 2 (over core), expert: 4 (over z), tp: 4 (over y, x).
Axes of the slice: x: 2, y: 2, z: 4, core: 2. Of those that a mesh axis runs over, the one named last changes fastest.
Arguments:
- tokens: bfloat16 [512, 4096], P('expert', ('tp', 'section')), may hold values from -6 to 6
- out_grad: bfloat16 [512, 4096], P('expert', ('tp', 'section')), may hold values from -12 to 12
- expert_ids: int32 [512, 2], P('expert'), may hold values from 0 to 3, all different within a row; in each aligned block of 128 rows (0 to 127, 128 to 255, ...) at most 72 rows name the same one
- combine: float32 [512, 2], P('expert'), may hold values from 0.05 to 0.5
- w_gate: bfloat16 [4, 4096, 768], P('expert', 'tp', 'section'), may hold values from -0.09375 to 0.09375
- w_up: bfloat16 [4, 4096, 768], P('expert', 'tp', 'section'), may hold values from -0.09375 to 0.09375
- w_down: bfloat16 [4, 768, 4096], P('expert', 'section', 'tp'), may hold values from -0.21875 to 0.21875
Outputs:
- token_grad: bfloat16 [512, 4096], P('expert', ('tp', 'section'))
- gate_weight_grad: bfloat16 [4, 4096, 768], P('expert', 'tp', 'section')
- up_weight_grad: bfloat16 [4, 4096, 768], P('expert', 'tp', 'section')
- down_weight_grad: bfloat16 [4, 768, 4096], P('expert', 'section', 'tp')
The draws below stay inside these ranges and needn't reach their ends.
Inputs may be any that keep to these rules, and one draw needn't show every extreme that they name: `expert_ids`: each row names 2 different experts; among the 128 rows of one index of expert no expert is named more than 72 times, a bound that some block reaches.
All inputs are finite; a program needn't handle non-finite values.
Results may differ from the reference program's by a relative error of at most 0.025.
Values may be sent and summed in bfloat16 or wider, within the bound.
A program may use at most 64 MiB of HBM per device.

```python
import math
import jax
import jax.numpy as jnp
import numpy as np
from jax import lax

D = 4096
FF = 768
TOK_DEV = 128
EXPERTS = 4
TOP = 2
CAP = 72
TOKENS = 512
N_SECTION = 2
N_EXPERT = 4
N_TP = 4


def block_scale(key, extent, shards, least, high):
    def one(position, parts):
        steps = jax.random.uniform(jax.random.fold_in(jax.random.fold_in(key, 6), position), (parts,), jnp.float32, least / len(shards), high / len(shards))
        return jnp.repeat(jnp.exp(steps), extent[position] // parts).reshape((-1,) + (1,) * (len(extent) - position - 1))

    loudness = one(*shards[0])
    for cut in shards[1:]:
        loudness = loudness * one(*cut)
    return loudness


def routed_block(rng, own, number, rows, count, top, reach, slope):
    sequence = jax.random.permutation(rng, count)
    heavy_load, usual = load_shares(count, rows * top, reach, slope, True), load_shares(count, rows * top, reach, slope, False)
    places = jnp.arange(count)

    def named(tallies, turn):
        used = int((tallies > 0).sum())
        fixed = max(1, used // 4)
        moved = fixed + (places - fixed + turn * (used - fixed)) % max(1, count - fixed)
        return jnp.zeros((count,), jnp.int32).at[sequence[jnp.where(places < fixed, places, moved)]].set(jnp.asarray(tallies, jnp.int32))

    tallies = jnp.where(number % 4 == 0, named(heavy_load, number // 4), named(usual, number - number // 4 - 1))
    mixed = jax.random.permutation(jax.random.fold_in(own, 3), count)
    giver, receiver = mixed[0:count // 2 * 2:2], mixed[1:count // 2 * 2:2]
    room = jnp.minimum(tallies[giver] - 1, reach - tallies[receiver]) // 2
    room = jnp.where((giver == sequence[0]) | (receiver == sequence[0]) | (tallies[receiver] == 0), 0, jnp.maximum(room, 0))
    moved = jax.random.randint(jax.random.fold_in(own, 4), (count // 2,), 0, 1 << 20) % (room + 1)
    tallies = tallies.at[giver].add(-moved).at[receiver].add(moved)
    labels = jnp.searchsorted(jnp.cumsum(tallies), jnp.arange(rows * top), side="right").astype(jnp.int32)
    grid = labels.reshape(top, rows).T
    grid = grid[jax.random.permutation(jax.random.fold_in(own, 1), rows)]
    turn = jax.random.randint(jax.random.fold_in(own, 2), (rows, 1), 0, top)
    return jnp.take_along_axis(grid, (jnp.arange(top)[None, :] + turn) % top, axis=1)


def load_shares(amount, total, most, slope, full):
    weights = [(1 << 20) // math.isqrt(grade ** slope) + 1 for grade in range(1, amount + 1)]
    largest = most if full else min(most, max(-(-total // amount), total * weights[0] // sum(weights)))
    least = 1 if total - largest >= amount - 1 else 0
    holding, surplus = [largest] + [least] * (amount - 1), total - largest - least * (amount - 1)
    while surplus > 0:
        free = [i for i in range(1, amount) if holding[i] < largest] or [i for i in range(1, amount) if holding[i] < most]
        mass, remaining = sum([weights[i] for i in free]), surplus
        for i in free:
            extra = min(most - holding[i], max(1, remaining * weights[i] // mass), surplus)
            holding[i] = holding[i] + extra
            surplus = surplus - extra
    return np.array(holding)


def scatter_about(stream_key, extent, width, limit, shards=(), kind=jnp.bfloat16):
    drawn = jax.random.normal(stream_key, extent, jnp.float32) * width
    if len(shards) > 0:
        drawn = block_scale(stream_key, extent, shards, -0.22, 0.18) * drawn
    return jnp.clip(drawn, min=-limit, max=limit).astype(kind)


def setup_inputs(seed: int = 0) -> dict:
    keys = jax.random.split(jax.random.key(seed), 8)
    tokens = scatter_about(keys[0], (TOKENS, D), 1.0, 6.0, ((0, 4), (1, 8)))
    out_grad = scatter_about(keys[1], (TOKENS, D), 2.0, 12.0, ((0, 4), (1, 8)))
    expert_ids_keys = jax.random.split(jax.random.fold_in(keys[2], 1), TOKENS // TOK_DEV)
    expert_ids_turns = jax.random.permutation(jax.random.fold_in(keys[2], 3), TOKENS // TOK_DEV)
    expert_ids = jax.vmap(lambda own, number: routed_block(jax.random.fold_in(keys[2], 2), own, number, TOK_DEV, EXPERTS, TOP, CAP, 2))(expert_ids_keys, expert_ids_turns).reshape((TOKENS, TOP))
    combine = jnp.clip(jnp.exp(math.log(0.5) - 2.3025851 * jax.random.uniform(keys[3], (TOKENS, TOP), jnp.float32) ** block_scale(keys[3], (TOKENS, TOP), ((0, 4),), -0.2, 0.2)), 0.05, 0.5)
    w_gate = scatter_about(keys[4], (EXPERTS, D, FF), D ** -0.5, 0.09375, ((0, 4), (1, 4), (2, 2)))
    w_up = scatter_about(keys[5], (EXPERTS, D, FF), D ** -0.5, 0.09375, ((0, 4), (1, 4), (2, 2)))
    w_down = scatter_about(keys[6], (EXPERTS, FF, D), FF ** -0.5, 0.21875, ((0, 4), (1, 2), (2, 4)))
    return {"tokens": tokens, "out_grad": out_grad, "expert_ids": expert_ids, "combine": combine, "w_gate": w_gate, "w_up": w_up, "w_down": w_down}


def block_slots(block_ids):
    flat_ids = block_ids.reshape(-1)
    pick_count = flat_ids.shape[0]
    onehot = (flat_ids[:, None] == jnp.arange(EXPERTS, dtype=jnp.int32)[None, :]).astype(jnp.int32)
    earlier = jnp.cumsum(onehot, axis=0) - onehot
    slot_index = jnp.sum(earlier * onehot, axis=1)
    place_index = flat_ids * CAP + slot_index
    source = jnp.zeros((EXPERTS * CAP,), jnp.int32).at[place_index].set(jnp.arange(pick_count, dtype=jnp.int32))
    filled = jnp.zeros((EXPERTS * CAP,), jnp.int32).at[place_index].set(jnp.ones((pick_count,), jnp.int32))
    return source.reshape(EXPERTS, CAP), filled.reshape(EXPERTS, CAP)


def round_back(values):
    return lax.optimization_barrier(values.astype(jnp.bfloat16)).astype(jnp.float32)


def reference(tokens, out_grad, expert_ids, combine, w_gate, w_up, w_down):
    sources, filled = jax.vmap(block_slots)(expert_ids.reshape(N_EXPERT, TOK_DEV, TOP))
    offsets = (jnp.arange(N_EXPERT, dtype=jnp.int32) * (TOK_DEV * TOP))[:, None]
    flat_weights = combine.reshape(-1)
    quarter = D // N_TP
    half_ff = FF // N_SECTION
    rows_total = N_EXPERT * CAP

    def one_expert(total_grad, expert):
        picks = (sources[:, expert, :] + offsets).reshape(-1)
        live_slot = filled[:, expert, :].reshape(-1)
        token_index = picks // TOP
        keep_mask = (live_slot > 0)[:, None]
        rows_in = jnp.where(keep_mask, tokens[token_index], jnp.zeros((), jnp.bfloat16))
        scaled = out_grad[token_index].astype(jnp.float32) * flat_weights[picks][:, None]
        grad_in = jnp.where(keep_mask, scaled, jnp.zeros((), jnp.float32)).astype(jnp.bfloat16)
        gate_w = w_gate[expert]
        up_w = w_up[expert]
        down_w = w_down[expert]
        rows_q = rows_in.astype(jnp.float32).reshape(rows_total, N_TP, quarter)
        grad_q = grad_in.astype(jnp.float32).reshape(rows_total, N_TP, quarter)
        gate_pre = jnp.sum(round_back(jnp.einsum("rqd,qdf->qrf", rows_q, gate_w.astype(jnp.float32).reshape(N_TP, quarter, FF))), axis=0)
        up_pre = jnp.sum(round_back(jnp.einsum("rqd,qdf->qrf", rows_q, up_w.astype(jnp.float32).reshape(N_TP, quarter, FF))), axis=0)
        hidden_grad = jnp.sum(round_back(jnp.einsum("rqd,fqd->qrf", grad_q, down_w.astype(jnp.float32).reshape(FF, N_TP, quarter))), axis=0)
        sigmoid_g = jax.nn.sigmoid(gate_pre)
        activated = (gate_pre * sigmoid_g * up_pre).astype(jnp.bfloat16)
        gate_grad = (hidden_grad * up_pre * sigmoid_g * (1.0 + gate_pre * (1.0 - sigmoid_g))).astype(jnp.bfloat16)
        up_grad = (hidden_grad * gate_pre * sigmoid_g).astype(jnp.bfloat16)
        down_wgrad = jnp.dot(activated.T, grad_in, preferred_element_type=jnp.float32).astype(jnp.bfloat16)
        gate_wgrad = jnp.dot(rows_in.T, gate_grad, preferred_element_type=jnp.float32).astype(jnp.bfloat16)
        up_wgrad = jnp.dot(rows_in.T, up_grad, preferred_element_type=jnp.float32).astype(jnp.bfloat16)
        row_grad = jnp.zeros((rows_total, D), jnp.float32)
        for index in range(N_SECTION):
            low = index * half_ff
            high = low + half_ff
            half_part = jnp.dot(gate_grad[:, low:high], gate_w[:, low:high].T, preferred_element_type=jnp.float32)
            half_part = half_part + jnp.dot(up_grad[:, low:high], up_w[:, low:high].T, preferred_element_type=jnp.float32)
            row_grad = row_grad + round_back(half_part)
        row_grad = jnp.where(keep_mask, row_grad, jnp.zeros((), jnp.float32))
        total_grad = total_grad.at[token_index].add(row_grad)
        return total_grad, (gate_wgrad, up_wgrad, down_wgrad)

    total_grad, stacked = lax.scan(one_expert, jnp.zeros((TOKENS, D), jnp.float32), jnp.arange(EXPERTS, dtype=jnp.int32))
    return total_grad.astype(jnp.bfloat16), stacked[0], stacked[1], stacked[2]
```

```python
import functools

import jax
import jax.numpy as jnp
from jax import lax
from jax.experimental import pallas as pl
from jax.experimental.pallas import tpu as pltpu
from jax.sharding import PartitionSpec as P

MESH = pl.DeviceIdType.MESH


def block_slots(expert_ids, experts, capacity):
    flat_ids = expert_ids.reshape(-1)
    pick_count = flat_ids.shape[0]
    onehot = (flat_ids[:, None] == jnp.arange(experts, dtype=jnp.int32)[None, :]).astype(jnp.int32)
    earlier = jnp.cumsum(onehot, axis=0) - onehot
    slot_index = jnp.sum(earlier * onehot, axis=1)
    place_index = flat_ids * capacity + slot_index
    source = (
        jnp.zeros((experts * capacity,), jnp.int32)
        .at[place_index]
        .set(jnp.arange(pick_count, dtype=jnp.int32))
    )
    filled = (
        jnp.zeros((experts * capacity,), jnp.int32)
        .at[place_index]
        .set(jnp.ones((pick_count,), jnp.int32))
    )
    return (slot_index, source.reshape(experts, capacity), filled.reshape(experts, capacity))


def round_back(values):
    return lax.optimization_barrier(values.astype(jnp.bfloat16)).astype(jnp.float32)


def local_grads(gate_pre, up_pre, hidden_grad):
    sigmoid_g = jax.nn.sigmoid(gate_pre)
    activated = (gate_pre * sigmoid_g * up_pre).astype(jnp.bfloat16)
    gate_grad = (hidden_grad * up_pre * sigmoid_g * (1.0 + gate_pre * (1.0 - sigmoid_g))).astype(
        jnp.bfloat16
    )
    up_grad = (hidden_grad * gate_pre * sigmoid_g).astype(jnp.bfloat16)
    return (activated, gate_grad, up_grad)


def fill_buffers(source, filled, combine, top_count, features, grad_rows):
    tok_count = features.shape[0]
    token_index = source // top_count
    keep_mask = (filled > 0)[:, :, None]
    positions = jnp.arange(tok_count, dtype=jnp.int32)[None, None, :]
    selector = jnp.logical_and(token_index[:, :, None] == positions, keep_mask).astype(jnp.bfloat16)
    rows_in = jnp.einsum(
        "ect,td->ecd", selector, features, preferred_element_type=jnp.float32
    ).astype(jnp.bfloat16)
    picked_grad = jnp.einsum("ect,td->ecd", selector, grad_rows, preferred_element_type=jnp.float32)
    weight = combine.reshape(-1)[source]
    grad_in = (picked_grad * weight[:, :, None]).astype(jnp.bfloat16)
    return (rows_in, grad_in)


def token_picker(pick_rows, tok_dev, top_count, row_count):
    columns = jnp.arange(row_count, dtype=jnp.int32)[None, None, :]
    hits = (pick_rows.reshape(tok_dev, top_count)[:, :, None] == columns).astype(jnp.int32)
    return jnp.sum(hits, axis=1)


def contract_rows(left_side, right_side):
    return lax.dot_general(
        left_side, right_side, (((0,), (0,)), ((), ())), preferred_element_type=jnp.float32
    )


def contract_last(left_side, right_side):
    return lax.dot_general(
        left_side, right_side, (((1,), (1,)), ((), ())), preferred_element_type=jnp.float32
    )


def on_device(tokens, out_grad, expert_ids, combine, w_gate, w_up, w_down):
    tok_dev, top_count = expert_ids.shape
    experts = lax.axis_size("expert")
    capacity = (tok_dev * top_count * 9 + 8 * experts - 1) // (8 * experts)
    slot_index, source, filled = block_slots(expert_ids, experts, capacity)
    features, grad_rows = (
        lax.all_gather(tokens, "section", axis=1, tiled=True),
        lax.all_gather(out_grad, "section", axis=1, tiled=True),
    )
    send_rows, send_grads = fill_buffers(source, filled, combine, top_count, features, grad_rows)
    got_rows, got_grads = (
        lax.all_to_all(send_rows, "expert", split_axis=0, concat_axis=0, tiled=True),
        lax.all_to_all(send_grads, "expert", split_axis=0, concat_axis=0, tiled=True),
    )
    width_dev = got_rows.shape[2]
    rows_in = got_rows.reshape(-1, width_dev)
    grad_in = got_grads.reshape(-1, width_dev)
    gate_w = w_gate[0]
    up_w = w_up[0]
    down_w = w_down[0]
    gate_part = round_back(jnp.dot(rows_in, gate_w, preferred_element_type=jnp.float32))
    up_part = round_back(jnp.dot(rows_in, up_w, preferred_element_type=jnp.float32))
    hidden_part = round_back(contract_last(grad_in, down_w))
    gate_pre, up_pre, hidden_grad = (
        lax.psum(gate_part.astype(jnp.bfloat16), "tp").astype(jnp.float32),
        lax.psum(up_part.astype(jnp.bfloat16), "tp").astype(jnp.float32),
        lax.psum(hidden_part.astype(jnp.bfloat16), "tp").astype(jnp.float32),
    )
    activated, gate_grad, up_grad = local_grads(gate_pre, up_pre, hidden_grad)
    row_float = contract_last(gate_grad, gate_w) + contract_last(up_grad, up_w)
    flat_ids = expert_ids.reshape(-1)
    pick_rows = flat_ids * capacity + slot_index
    picker = token_picker(pick_rows, tok_dev, top_count, experts * capacity)
    row_grad = row_float.astype(jnp.bfloat16)
    returned = lax.all_to_all(
        row_grad.reshape(experts, capacity, width_dev),
        "expert",
        split_axis=0,
        concat_axis=0,
        tiled=True,
    )
    summed = jnp.dot(
        picker.astype(jnp.bfloat16),
        returned.reshape(experts * capacity, width_dev),
        preferred_element_type=jnp.float32,
    )
    token_grad = lax.psum_scatter(
        summed.astype(jnp.bfloat16), "section", scatter_dimension=1, tiled=True
    )
    down_wgrad = contract_rows(activated, grad_in).astype(jnp.bfloat16)[None]
    gate_wgrad = contract_rows(rows_in, gate_grad).astype(jnp.bfloat16)[None]
    up_wgrad = contract_rows(rows_in, up_grad).astype(jnp.bfloat16)[None]
    return (token_grad, gate_wgrad, up_wgrad, down_wgrad)


def expert_kernel(
    n,
    slots,
    tok_ref,
    grad_ref,
    ids_ref,
    combine_ref,
    gate_hbm,
    up_hbm,
    down_hbm,
    token_out,
    gate_out,
    up_out,
    down_out,
    gate_w,
    up_w,
    down_w,
    picks,
    send_rows,
    send_grads,
    rows,
    grads,
    parts,
    got_parts,
    local,
    halves,
    got_half,
    back,
    returned,
    gate_g,
    up_g,
    down_g,
    io_sem,
    z_send,
    z_recv,
    s_send,
    s_recv,
    p_send,
    p_recv,
    a_send,
    a_recv,
    h_send,
    h_recv,
    r_send,
    r_recv,
):
    sec = lax.axis_index("section")
    exp = lax.axis_index("expert")
    tp = lax.axis_index("tp")
    other = 1 - sec
    tok_dev, width = tok_ref.shape
    hidden = gate_w.shape[1]

    def hop(axis, index):
        place = {"section": sec, "expert": exp, "tp": tp}
        place[axis] = index
        return (place["section"], place["expert"], place["tp"])

    def remote(src, dst, send, recv, target):
        return pltpu.make_async_remote_copy(
            src_ref=src,
            dst_ref=dst,
            send_sem=send,
            recv_sem=recv,
            device_id=target,
            device_id_type=MESH,
        )

    loads = [
        pltpu.make_async_copy(src, dst, io_sem.at[index])
        for index, (src, dst) in enumerate(((gate_hbm, gate_w), (up_hbm, up_w), (down_hbm, down_w)))
    ]
    for load in loads:
        load.start()

    barrier = pltpu.get_barrier_semaphore()
    pl.semaphore_signal(barrier, inc=1, device_id=hop("section", other), device_id_type=MESH)
    for step in range(1, n):
        pl.semaphore_signal(
            barrier, inc=1, device_id=hop("expert", lax.rem(exp + step, n)), device_id_type=MESH
        )
        pl.semaphore_signal(
            barrier, inc=1, device_id=hop("tp", lax.rem(tp + step, n)), device_id_type=MESH
        )

    target = lax.rem(exp + lax.broadcasted_iota(jnp.int32, (tok_dev, 128), 1), n)
    first = ids_ref[:, 0:1] == target
    second = ids_ref[:, 1:2] == target
    named = jnp.logical_or(first, second).astype(jnp.float32)
    weight = jnp.where(first, combine_ref[:, 0:1], 0.0) + jnp.where(second, combine_ref[:, 1:2], 0.0)
    earlier = (
        lax.broadcasted_iota(jnp.int32, (tok_dev, tok_dev), 1)
        < lax.broadcasted_iota(jnp.int32, (tok_dev, tok_dev), 0)
    ).astype(jnp.bfloat16)
    slot = jnp.dot(earlier, named.astype(jnp.bfloat16), preferred_element_type=jnp.float32)
    place = jnp.where(named > 0.0, slot, -1.0)
    columns = lax.broadcasted_iota(jnp.int32, (tok_dev, slots), 1).astype(jnp.float32)
    tokens = tok_ref[...]
    out_grad = grad_ref[...].astype(jnp.float32)

    def block(d):
        return pl.ds(d * slots, slots)

    def z_copies(d):
        goal = hop("expert", lax.rem(exp + d, n))
        return (
            remote(send_rows.at[d - 1], rows.at[sec, block(d)], z_send.at[0, d - 1], z_recv.at[0, d - 1], goal),
            remote(send_grads.at[d - 1], grads.at[sec, block(d)], z_send.at[1, d - 1], z_recv.at[1, d - 1], goal),
        )

    def s_copies(d):
        goal = hop("section", other)
        return (
            remote(rows.at[sec, block(d)], rows.at[sec, block(d)], s_send.at[0, d], s_recv.at[0, d], goal),
            remote(grads.at[sec, block(d)], grads.at[sec, block(d)], s_send.at[1, d], s_recv.at[1, d], goal),
        )

    order = [2, 1, 3, 0] if n == 4 else list(range(1, n)) + [0]
    for turn, d in enumerate(order):
        pick = (place[:, d : d + 1] == columns).astype(jnp.bfloat16)
        picks[d] = pick
        picked = contract_rows(pick, tokens).astype(jnp.bfloat16)
        scaled = (out_grad * weight[:, d : d + 1]).astype(jnp.bfloat16)
        picked_grad = contract_rows(pick, scaled).astype(jnp.bfloat16)
        if d == 0:
            rows[sec, block(0)] = picked
            grads[sec, block(0)] = picked_grad
            for copy in s_copies(0):
                copy.start()
        else:
            send_rows[d - 1] = picked
            send_grads[d - 1] = picked_grad
            if turn == 0:
                pl.semaphore_wait(barrier, 2 * n - 1)
            for copy in z_copies(d):
                copy.start()

    for load in loads:
        load.wait()

    def p_copy(d):
        slot_there = lax.rem(tp - d + n, n) - 1
        return remote(
            parts.at[d], got_parts.at[slot_there], p_send.at[d], p_recv.at[slot_there], hop("tp", d)
        )

    arrivals = [0, 1, 3, 2] if n == 4 else list(range(n))
    for d in arrivals:
        if d != 0:
            for copy, onward in zip(z_copies(d), s_copies(d)):
                copy.wait_recv()
                onward.start()
        for copy in s_copies(d):
            copy.wait_recv()
        for index, weights in ((0, gate_w), (1, up_w)):
            total = jnp.dot(rows[0, block(d)], weights[0:width, :], preferred_element_type=jnp.float32)
            total += jnp.dot(rows[1, block(d)], weights[width : 2 * width, :], preferred_element_type=jnp.float32)
            parts[d, :, index * hidden : (index + 1) * hidden] = total.astype(jnp.bfloat16)
        total = contract_last(grads[0, block(d)], down_w[:, 0:width])
        total += contract_last(grads[1, block(d)], down_w[:, width : 2 * width])
        parts[d, :, 2 * hidden : 3 * hidden] = total.astype(jnp.bfloat16)

        @pl.when(tp != d)
        def _():
            p_copy(d).start()

    def p_arrival(k):
        return remote(parts.at[0], got_parts.at[k], p_send.at[0], p_recv.at[k], hop("tp", lax.rem(tp + 1, n)))

    summed = parts[tp].astype(jnp.float32)
    for k in range(n - 1):
        p_arrival(k).wait_recv()
        summed += got_parts[k].astype(jnp.float32)
    activated, gate_grad, up_grad = local_grads(
        summed[:, 0:hidden], summed[:, hidden : 2 * hidden], summed[:, 2 * hidden : 3 * hidden]
    )
    local[tp, :, 0:hidden] = gate_grad
    local[tp, :, hidden : 2 * hidden] = up_grad
    local[tp, :, 2 * hidden : 3 * hidden] = activated

    def a_copy(k):
        return remote(
            local.at[tp], local.at[tp], a_send.at[k - 1], a_recv.at[k - 1], hop("tp", lax.rem(tp + k, n))
        )

    for k in (2, 1, 3) if n == 4 else range(1, n):
        a_copy(k).start()

    def h_copy(k):
        return remote(halves.at[k], got_half.at[k], h_send.at[k], h_recv.at[k], hop("section", other))

    def r_copy(k, p):
        return remote(
            back.at[k],
            returned.at[p],
            r_send.at[k],
            r_recv.at[p],
            hop("expert", lax.rem(exp - p + n, n)),
        )

    for k in (0, 1, 3, 2) if n == 4 else range(n):
        p = lax.rem(tp - k + n, n)
        if k > 0:
            a_copy(k).wait_recv()
        gate_grad = local[p, :, 0:hidden]
        up_grad = local[p, :, hidden : 2 * hidden]

        def row_part(side):
            span = pl.ds(pl.multiple_of(side * width, width), width)
            total = contract_last(gate_grad, gate_w[span, :])
            return total + contract_last(up_grad, up_w[span, :])

        halves[k] = row_part(other).astype(jnp.bfloat16)
        h_copy(k).start()
        own = row_part(sec)
        h_copy(k).wait_recv()
        whole = (own + got_half[k].astype(jnp.float32)).astype(jnp.bfloat16)

        @pl.when(p == 0)
        def _():
            returned[0] = whole

        @pl.when(p != 0)
        def _():
            back[k] = whole
            r_copy(k, p).start()

    total_rows = n * slots
    every = local[...].reshape(total_rows, 3 * hidden)
    chunk = 256
    stores = []
    for index, (result, out) in enumerate(((gate_g, gate_out), (up_g, up_out))):
        for side in range(2):
            for low in range(0, width, chunk):
                left = rows[side, :, low : low + chunk]
                start = side * width + low
                result[start : start + chunk, :] = sum(contract_rows(rows[side, block(d), low : low + chunk], local[d, :, index * hidden : (index + 1) * hidden]) for d in range(n)).astype(jnp.bfloat16)
        store = pltpu.make_async_copy(result, out, io_sem.at[3 + index])
        store.start()
        stores.append(store)
    right = every[:, 2 * hidden : 3 * hidden]
    for side in range(2):
        for low in range(0, width, chunk):
            start = side * width + low
            down_g[:, start : start + chunk] = contract_rows(
                right, grads[side, :, low : low + chunk]
            ).astype(jnp.bfloat16)
    store = pltpu.make_async_copy(down_g, down_out, io_sem.at[5])
    store.start()
    stores.append(store)

    total = jnp.dot(picks[0], returned[0], preferred_element_type=jnp.float32)
    for d in (1, 3, 2) if n == 4 else range(1, n):
        remote(back.at[0], returned.at[d], r_send.at[0], r_recv.at[d], hop("expert", lax.rem(exp + 1, n))).wait_recv()
        total += jnp.dot(picks[d], returned[d], preferred_element_type=jnp.float32)
    token_out[...] = total.astype(jnp.bfloat16)

    for d in range(1, n):
        for copy in z_copies(d):
            copy.wait_send()
        a_copy(d).wait_send()
    for d in range(n):
        for copy in s_copies(d):
            copy.wait_send()
        h_copy(d).wait_send()

        @pl.when(tp != d)
        def _():
            p_copy(d).wait_send()

        p = lax.rem(tp - d + n, n)

        @pl.when(p != 0)
        def _():
            r_copy(d, p).wait_send()

    for store in stores:
        store.wait()


def on_device_kernel(tokens, out_grad, expert_ids, combine, w_gate, w_up, w_down):
    tok_dev, top_count = expert_ids.shape
    n = lax.axis_size("expert")
    capacity = (tok_dev * top_count * 9 + 8 * n - 1) // (8 * n)
    slots = (capacity + 15) // 16 * 16
    width = tokens.shape[1]
    depth, hidden = w_gate.shape[1:]
    bf16 = jnp.bfloat16
    vmem = pl.BlockSpec(memory_space=pltpu.VMEM)
    hbm = pl.BlockSpec(memory_space=pl.ANY)
    dma = pltpu.SemaphoreType.DMA
    token_grad, gate_g, up_g, down_g = pl.pallas_call(
        functools.partial(expert_kernel, n, slots),
        out_shape=(
            jax.ShapeDtypeStruct((tok_dev, width), bf16),
            jax.ShapeDtypeStruct((depth, hidden), bf16),
            jax.ShapeDtypeStruct((depth, hidden), bf16),
            jax.ShapeDtypeStruct((hidden, depth), bf16),
        ),
        in_specs=[vmem, vmem, vmem, vmem, hbm, hbm, hbm],
        out_specs=(vmem, hbm, hbm, hbm),
        scratch_shapes=[
            pltpu.VMEM((depth, hidden), bf16),
            pltpu.VMEM((depth, hidden), bf16),
            pltpu.VMEM((hidden, depth), bf16),
            pltpu.VMEM((n, tok_dev, slots), bf16),
            pltpu.VMEM((n - 1, slots, width), bf16),
            pltpu.VMEM((n - 1, slots, width), bf16),
            pltpu.VMEM((2, n * slots, width), bf16),
            pltpu.VMEM((2, n * slots, width), bf16),
            pltpu.VMEM((n, slots, 3 * hidden), bf16),
            pltpu.VMEM((n - 1, slots, 3 * hidden), bf16),
            pltpu.VMEM((n, slots, 3 * hidden), bf16),
            pltpu.VMEM((n, slots, width), bf16),
            pltpu.VMEM((n, slots, width), bf16),
            pltpu.VMEM((n, slots, width), bf16),
            pltpu.VMEM((n, slots, width), bf16),
            pltpu.VMEM((depth, hidden), bf16),
            pltpu.VMEM((depth, hidden), bf16),
            pltpu.VMEM((hidden, depth), bf16),
            dma((6,)),
            dma((2, n - 1)),
            dma((2, n - 1)),
            dma((2, n)),
            dma((2, n)),
            dma((n,)),
            dma((n - 1,)),
            dma((n - 1,)),
            dma((n - 1,)),
            dma((n,)),
            dma((n,)),
            dma((n,)),
            dma((n,)),
        ],
        compiler_params=pltpu.CompilerParams(
            collective_id=0, has_side_effects=True, vmem_limit_bytes=48 * 1024 * 1024
        ),
    )(tokens, out_grad, expert_ids, combine, w_gate[0], w_up[0], w_down[0])
    return (token_grad, gate_g[None], up_g[None], down_g[None])


def fits_kernel(mesh):
    shape = mesh.shape
    return shape["section"] == 2 and shape["expert"] == shape["tp"]


def solution(mesh):
    return jax.shard_map(
        on_device_kernel if fits_kernel(mesh) else on_device,
        mesh=mesh,
        in_specs=(
            P("expert", ("tp", "section")),
            P("expert", ("tp", "section")),
            P("expert", None),
            P("expert", None),
            P("expert", "tp", "section"),
            P("expert", "tp", "section"),
            P("expert", "section", "tp"),
        ),
        out_specs=(
            P("expert", ("tp", "section")),
            P("expert", "tp", "section"),
            P("expert", "tp", "section"),
            P("expert", "section", "tp"),
        ),
        check_vma=False,
    )
```

```python
import functools

import jax
import jax.numpy as jnp
from jax import lax
from jax.experimental import pallas as pl
from jax.experimental.pallas import tpu as pltpu
from jax.sharding import PartitionSpec as P

MESH = pl.DeviceIdType.MESH


def block_slots(expert_ids, experts, capacity):
    flat_ids = expert_ids.reshape(-1)
    pick_count = flat_ids.shape[0]
    onehot = (flat_ids[:, None] == jnp.arange(experts, dtype=jnp.int32)[None, :]).astype(jnp.int32)
    earlier = jnp.cumsum(onehot, axis=0) - onehot
    slot_index = jnp.sum(earlier * onehot, axis=1)
    place_index = flat_ids * capacity + slot_index
    source = (
        jnp.zeros((experts * capacity,), jnp.int32)
        .at[place_index]
        .set(jnp.arange(pick_count, dtype=jnp.int32))
    )
    filled = (
        jnp.zeros((experts * capacity,), jnp.int32)
        .at[place_index]
        .set(jnp.ones((pick_count,), jnp.int32))
    )
    return (slot_index, source.reshape(experts, capacity), filled.reshape(experts, capacity))


def round_back(values):
    return lax.optimization_barrier(values.astype(jnp.bfloat16)).astype(jnp.float32)


def local_grads(gate_pre, up_pre, hidden_grad):
    sigmoid_g = jax.nn.sigmoid(gate_pre)
    activated = (gate_pre * sigmoid_g * up_pre).astype(jnp.bfloat16)
    gate_grad = (hidden_grad * up_pre * sigmoid_g * (1.0 + gate_pre * (1.0 - sigmoid_g))).astype(
        jnp.bfloat16
    )
    up_grad = (hidden_grad * gate_pre * sigmoid_g).astype(jnp.bfloat16)
    return (activated, gate_grad, up_grad)


def fill_buffers(source, filled, combine, top_count, features, grad_rows):
    tok_count = features.shape[0]
    token_index = source // top_count
    keep_mask = (filled > 0)[:, :, None]
    positions = jnp.arange(tok_count, dtype=jnp.int32)[None, None, :]
    selector = jnp.logical_and(token_index[:, :, None] == positions, keep_mask).astype(jnp.bfloat16)
    rows_in = jnp.einsum(
        "ect,td->ecd", selector, features, preferred_element_type=jnp.float32
    ).astype(jnp.bfloat16)
    picked_grad = jnp.einsum("ect,td->ecd", selector, grad_rows, preferred_element_type=jnp.float32)
    weight = combine.reshape(-1)[source]
    grad_in = (picked_grad * weight[:, :, None]).astype(jnp.bfloat16)
    return (rows_in, grad_in)


def token_picker(pick_rows, tok_dev, top_count, row_count):
    columns = jnp.arange(row_count, dtype=jnp.int32)[None, None, :]
    hits = (pick_rows.reshape(tok_dev, top_count)[:, :, None] == columns).astype(jnp.int32)
    return jnp.sum(hits, axis=1)


def contract_rows(left_side, right_side):
    return lax.dot_general(
        left_side, right_side, (((0,), (0,)), ((), ())), preferred_element_type=jnp.float32
    )


def contract_last(left_side, right_side):
    return lax.dot_general(
        left_side, right_side, (((1,), (1,)), ((), ())), preferred_element_type=jnp.float32
    )


def on_device(tokens, out_grad, expert_ids, combine, w_gate, w_up, w_down):
    tok_dev, top_count = expert_ids.shape
    experts = lax.axis_size("expert")
    capacity = (tok_dev * top_count * 9 + 8 * experts - 1) // (8 * experts)
    slot_index, source, filled = block_slots(expert_ids, experts, capacity)
    features, grad_rows = (
        lax.all_gather(tokens, "section", axis=1, tiled=True),
        lax.all_gather(out_grad, "section", axis=1, tiled=True),
    )
    send_rows, send_grads = fill_buffers(source, filled, combine, top_count, features, grad_rows)
    got_rows, got_grads = (
        lax.all_to_all(send_rows, "expert", split_axis=0, concat_axis=0, tiled=True),
        lax.all_to_all(send_grads, "expert", split_axis=0, concat_axis=0, tiled=True),
    )
    width_dev = got_rows.shape[2]
    rows_in = got_rows.reshape(-1, width_dev)
    grad_in = got_grads.reshape(-1, width_dev)
    gate_w = w_gate[0]
    up_w = w_up[0]
    down_w = w_down[0]
    gate_part = round_back(jnp.dot(rows_in, gate_w, preferred_element_type=jnp.float32))
    up_part = round_back(jnp.dot(rows_in, up_w, preferred_element_type=jnp.float32))
    hidden_part = round_back(contract_last(grad_in, down_w))
    gate_pre, up_pre, hidden_grad = (
        lax.psum(gate_part.astype(jnp.bfloat16), "tp").astype(jnp.float32),
        lax.psum(up_part.astype(jnp.bfloat16), "tp").astype(jnp.float32),
        lax.psum(hidden_part.astype(jnp.bfloat16), "tp").astype(jnp.float32),
    )
    activated, gate_grad, up_grad = local_grads(gate_pre, up_pre, hidden_grad)
    row_float = contract_last(gate_grad, gate_w) + contract_last(up_grad, up_w)
    flat_ids = expert_ids.reshape(-1)
    pick_rows = flat_ids * capacity + slot_index
    picker = token_picker(pick_rows, tok_dev, top_count, experts * capacity)
    row_grad = row_float.astype(jnp.bfloat16)
    returned = lax.all_to_all(
        row_grad.reshape(experts, capacity, width_dev),
        "expert",
        split_axis=0,
        concat_axis=0,
        tiled=True,
    )
    summed = jnp.dot(
        picker.astype(jnp.bfloat16),
        returned.reshape(experts * capacity, width_dev),
        preferred_element_type=jnp.float32,
    )
    token_grad = lax.psum_scatter(
        summed.astype(jnp.bfloat16), "section", scatter_dimension=1, tiled=True
    )
    down_wgrad = contract_rows(activated, grad_in).astype(jnp.bfloat16)[None]
    gate_wgrad = contract_rows(rows_in, gate_grad).astype(jnp.bfloat16)[None]
    up_wgrad = contract_rows(rows_in, up_grad).astype(jnp.bfloat16)[None]
    return (token_grad, gate_wgrad, up_wgrad, down_wgrad)


def expert_kernel(
    n,
    slots,
    tok_hbm,
    grad_hbm,
    ids_ref,
    combine_ref,
    gate_hbm,
    up_hbm,
    down_hbm,
    token_out,
    gate_out,
    up_out,
    down_out,
    tok_ref,
    grad_ref,
    both_w,
    down_w,
    picks,
    send_rows,
    send_grads,
    rows,
    grads,
    parts,
    got_parts,
    local,
    halves,
    got_half,
    back,
    returned,
    gate_g,
    up_g,
    down_g,
    io_sem,
    z_send,
    z_recv,
    s_send,
    s_recv,
    p_send,
    p_recv,
    a_send,
    a_recv,
    h_send,
    h_recv,
    r_send,
    r_recv,
):
    sec = lax.axis_index("section")
    exp = lax.axis_index("expert")
    tp = lax.axis_index("tp")
    other = 1 - sec
    tok_dev, width = tok_ref.shape
    hidden = down_w.shape[0]
    groups = hidden // 128
    share = parts.shape[1] // n
    sign = 2 * lax.rem(exp, 2) - 1

    def hop(axis, index):
        place = {"section": sec, "expert": exp, "tp": tp}
        place[axis] = index
        return (place["section"], place["expert"], place["tp"])

    def remote(src, dst, send, recv, target):
        return pltpu.make_async_remote_copy(
            src_ref=src,
            dst_ref=dst,
            send_sem=send,
            recv_sem=recv,
            device_id=target,
            device_id_type=MESH,
        )

    def partner(k):
        return lax.rem(exp + n + sign * k, n)

    fetch = [
        pltpu.make_async_copy(tok_hbm, tok_ref, io_sem.at[0]),
        pltpu.make_async_copy(grad_hbm, grad_ref, io_sem.at[1]),
    ]
    loads = [pltpu.make_async_copy(down_hbm, down_w, io_sem.at[2])]
    for j in range(groups):
        for index, source in enumerate((gate_hbm, up_hbm)):
            loads.append(
                pltpu.make_async_copy(
                    source.at[:, pl.ds(j * 128, 128)],
                    both_w.at[:, pl.ds((2 * j + index) * 128, 128)],
                    io_sem.at[3 + 2 * j + index],
                )
            )
    for copy in fetch + loads:
        copy.start()

    barrier = pltpu.get_barrier_semaphore()
    pl.semaphore_signal(barrier, inc=1, device_id=hop("section", other), device_id_type=MESH)
    for k in range(1, n):
        pl.semaphore_signal(barrier, inc=1, device_id=hop("expert", partner(k)), device_id_type=MESH)
        pl.semaphore_signal(
            barrier, inc=1, device_id=hop("tp", lax.rem(tp + k, n)), device_id_type=MESH
        )

    target = lax.rem(exp + 2 * n + sign * lax.rem(lax.broadcasted_iota(jnp.int32, (8, tok_dev), 0), n), n)
    first = ids_ref[0:1, :] == target
    second = ids_ref[1:2, :] == target
    named = jnp.logical_or(first, second).astype(jnp.float32)
    weight = jnp.where(first, combine_ref[0:1, :], 0.0) + jnp.where(second, combine_ref[1:2, :], 0.0)
    earlier = (
        lax.broadcasted_iota(jnp.int32, (tok_dev, tok_dev), 0)
        < lax.broadcasted_iota(jnp.int32, (tok_dev, tok_dev), 1)
    ).astype(jnp.bfloat16)
    slot = jnp.dot(named.astype(jnp.bfloat16), earlier, preferred_element_type=jnp.float32)
    place = jnp.where(named > 0.0, slot, -1.0)
    numbers = lax.broadcasted_iota(jnp.int32, (slots, tok_dev), 0).astype(jnp.float32)
    spare = n * share - groups * slots
    if spare > 0:
        for k in range(n):
            parts[k, groups * slots :, :] = jnp.zeros((spare, 384), jnp.bfloat16)

    def block(k):
        return pl.ds(k * slots, slots)

    def z_copies(k):
        goal = hop("expert", partner(k))
        return (
            remote(send_rows.at[k - 1], rows.at[sec, block(k)], z_send.at[0, k - 1], z_recv.at[0, k - 1], goal),
            remote(send_grads.at[k - 1], grads.at[sec, block(k)], z_send.at[1, k - 1], z_recv.at[1, k - 1], goal),
        )

    def s_copies(k):
        goal = hop("section", other)
        return (
            remote(rows.at[sec, block(k)], rows.at[sec, block(k)], s_send.at[0, k], s_recv.at[0, k], goal),
            remote(grads.at[sec, block(k)], grads.at[sec, block(k)], s_send.at[1, k], s_recv.at[1, k], goal),
        )

    def p_copy(k, r):
        goal = lax.rem(tp + r, n)
        span = pl.ds(pl.multiple_of(goal * share, share), share)
        return remote(
            parts.at[k, span], got_parts.at[k, r - 1], p_send.at[k, r - 1], p_recv.at[k, r - 1], hop("tp", goal)
        )

    mine = pl.ds(pl.multiple_of(tp * share, share), share)

    def a_copy(k, r):
        return remote(
            local.at[k, mine], local.at[k, mine], a_send.at[k, r - 1], a_recv.at[k, r - 1], hop("tp", lax.rem(tp + r, n))
        )

    def h_copy(k):
        return remote(halves.at[k], got_half.at[k], h_send.at[k], h_recv.at[k], hop("section", other))

    def r_copy(k):
        return remote(back.at[k - 1], returned.at[k], r_send.at[k - 1], r_recv.at[k - 1], hop("expert", partner(k)))

    far_first = (2, 1, 3)

    for copy in fetch:
        copy.wait()
    for turn, k in enumerate((1, 2, 0, 3)):
        pick = (place[k : k + 1, :] == numbers).astype(jnp.float32)
        spread = jnp.sum(pick * weight[k : k + 1, :], axis=1, keepdims=True)
        pick = pick.astype(jnp.bfloat16)
        picks[k] = pick
        picked = jnp.dot(pick, tok_ref[...], preferred_element_type=jnp.float32).astype(jnp.bfloat16)
        if k == 0:
            rows[sec, block(0)] = picked
        else:
            send_rows[k - 1] = picked
            if turn == 0:
                pl.semaphore_wait(barrier, 2 * n - 1)
            z_copies(k)[0].start()
        picked_grad = jnp.dot(pick, grad_ref[...], preferred_element_type=jnp.float32)
        picked_grad = (picked_grad * spread).astype(jnp.bfloat16)
        if k == 0:
            grads[sec, block(0)] = picked_grad
            for copy in s_copies(0):
                copy.start()
        else:
            send_grads[k - 1] = picked_grad
            z_copies(k)[1].start()

    for load in loads:
        load.wait()

    def arrive(k):
        for copy, onward in zip(z_copies(k), s_copies(k)):
            copy.wait_recv()
            onward.start()

    def forward(k):
        for copy in s_copies(k):
            copy.wait_recv()
        pre = jnp.dot(rows[0, block(k)], both_w[0:width, :], preferred_element_type=jnp.float32)
        pre += jnp.dot(rows[1, block(k)], both_w[width : 2 * width, :], preferred_element_type=jnp.float32)
        inner = contract_last(grads[0, block(k)], down_w[:, 0:width])
        inner += contract_last(grads[1, block(k)], down_w[:, width : 2 * width])
        for j in range(groups):
            parts[k, j * slots : (j + 1) * slots, 0:256] = pre[:, j * 256 : (j + 1) * 256].astype(jnp.bfloat16)
            parts[k, j * slots : (j + 1) * slots, 256:384] = inner[:, j * 128 : (j + 1) * 128].astype(jnp.bfloat16)
        for r in far_first:
            p_copy(k, r).start()

    def reduce_local(k):
        summed = parts[k, mine, :].astype(jnp.float32)
        for r in range(1, n):
            p_copy(k, r).wait_recv()
            summed += got_parts[k, r - 1].astype(jnp.float32)
        activated, gate_grad, up_grad = local_grads(summed[:, 0:128], summed[:, 128:256], summed[:, 256:384])
        local[k, mine, 0:128] = gate_grad
        local[k, mine, 128:256] = up_grad
        local[k, mine, 256:384] = activated
        for r in far_first:
            a_copy(k, r).start()

    def row_side(k, side):
        span = pl.ds(pl.multiple_of(side * width, width), width)
        return contract_last(gate_up(k), both_w[span, :])

    def gate_up(k):
        return jnp.concatenate(
            [local[k, j * slots : (j + 1) * slots, 0:256] for j in range(groups)], axis=1
        )

    def active(k):
        return jnp.concatenate(
            [local[k, j * slots : (j + 1) * slots, 256:384] for j in range(groups)], axis=1
        )

    def backward(k):
        for r in range(1, n):
            a_copy(k, r).wait_recv()
        halves[k] = row_side(k, other).astype(jnp.bfloat16)
        h_copy(k).start()

    def give_back(k):
        own = row_side(k, sec)
        h_copy(k).wait_recv()
        whole = (own + got_half[k].astype(jnp.float32)).astype(jnp.bfloat16)
        if k == 0:
            returned[0] = whole
        else:
            back[k - 1] = whole
            r_copy(k).start()

    forward(0)
    arrive(1)
    reduce_local(0)
    forward(1)
    backward(0)
    arrive(3)
    reduce_local(1)
    forward(3)
    give_back(0)
    backward(1)
    arrive(2)
    give_back(1)
    forward(2)
    reduce_local(3)
    backward(3)
    give_back(3)
    reduce_local(2)
    backward(2)
    give_back(2)

    chunk = 256
    for side in range(2):
        for low in range(0, width, chunk):
            total = sum(
                contract_rows(rows[side, block(k), low : low + chunk], gate_up(k)) for k in range(n)
            ).astype(jnp.bfloat16)
            start = side * width + low
            for j in range(groups):
                gate_g[start : start + chunk, j * 128 : (j + 1) * 128] = total[:, j * 256 : j * 256 + 128]
                up_g[start : start + chunk, j * 128 : (j + 1) * 128] = total[:, j * 256 + 128 : (j + 1) * 256]
    stores = [
        pltpu.make_async_copy(gate_g, gate_out, io_sem.at[0]),
        pltpu.make_async_copy(up_g, up_out, io_sem.at[1]),
        pltpu.make_async_copy(down_g, down_out, io_sem.at[2]),
    ]
    stores[0].start()
    stores[1].start()
    for side in range(2):
        for low in range(0, width, chunk):
            start = side * width + low
            down_g[:, start : start + chunk] = sum(
                contract_rows(active(k), grads[side, block(k), low : low + chunk]) for k in range(n)
            ).astype(jnp.bfloat16)
    stores[2].start()

    total = contract_rows(picks[0], returned[0])
    for k in (1, 3, 2):
        r_copy(k).wait_recv()
        total += contract_rows(picks[k], returned[k])
    token_out[...] = total.astype(jnp.bfloat16)

    for k in range(n):
        for copy in s_copies(k):
            copy.wait_send()
        h_copy(k).wait_send()
        for r in range(1, n):
            p_copy(k, r).wait_send()
            a_copy(k, r).wait_send()
        if k > 0:
            for copy in z_copies(k):
                copy.wait_send()
            r_copy(k).wait_send()
    for store in stores:
        store.wait()


def on_device_kernel(tokens, out_grad, expert_ids, combine, w_gate, w_up, w_down):
    tok_dev, top_count = expert_ids.shape
    n = lax.axis_size("expert")
    capacity = (tok_dev * top_count * 9 + 8 * n - 1) // (8 * n)
    slots = (capacity + 15) // 16 * 16
    width = tokens.shape[1]
    depth, hidden = w_gate.shape[1:]
    groups = hidden // 128
    share = (groups * slots + 16 * n - 1) // (16 * n) * 16
    bf16 = jnp.bfloat16
    vmem = pl.BlockSpec(memory_space=pltpu.VMEM)
    hbm = pl.BlockSpec(memory_space=pl.ANY)
    dma = pltpu.SemaphoreType.DMA
    token_grad, gate_g, up_g, down_g = pl.pallas_call(
        functools.partial(expert_kernel, n, slots),
        out_shape=(
            jax.ShapeDtypeStruct((tok_dev, width), bf16),
            jax.ShapeDtypeStruct((depth, hidden), bf16),
            jax.ShapeDtypeStruct((depth, hidden), bf16),
            jax.ShapeDtypeStruct((hidden, depth), bf16),
        ),
        in_specs=[hbm, hbm, vmem, vmem, hbm, hbm, hbm],
        out_specs=(vmem, hbm, hbm, hbm),
        scratch_shapes=[
            pltpu.VMEM((tok_dev, width), bf16),
            pltpu.VMEM((tok_dev, width), bf16),
            pltpu.VMEM((depth, 2 * hidden), bf16),
            pltpu.VMEM((hidden, depth), bf16),
            pltpu.VMEM((n, slots, tok_dev), bf16),
            pltpu.VMEM((n - 1, slots, width), bf16),
            pltpu.VMEM((n - 1, slots, width), bf16),
            pltpu.VMEM((2, n * slots, width), bf16),
            pltpu.VMEM((2, n * slots, width), bf16),
            pltpu.VMEM((n, n * share, 384), bf16),
            pltpu.VMEM((n, n - 1, share, 384), bf16),
            pltpu.VMEM((n, n * share, 384), bf16),
            pltpu.VMEM((n, slots, width), bf16),
            pltpu.VMEM((n, slots, width), bf16),
            pltpu.VMEM((n - 1, slots, width), bf16),
            pltpu.VMEM((n, slots, width), bf16),
            pltpu.VMEM((depth, hidden), bf16),
            pltpu.VMEM((depth, hidden), bf16),
            pltpu.VMEM((hidden, depth), bf16),
            dma((3 + 2 * groups,)),
            dma((2, n - 1)),
            dma((2, n - 1)),
            dma((2, n)),
            dma((2, n)),
            dma((n, n - 1)),
            dma((n, n - 1)),
            dma((n, n - 1)),
            dma((n, n - 1)),
            dma((n,)),
            dma((n,)),
            dma((n - 1,)),
            dma((n - 1,)),
        ],
        compiler_params=pltpu.CompilerParams(
            collective_id=0, has_side_effects=True, vmem_limit_bytes=48 * 1024 * 1024
        ),
    )(tokens, out_grad, expert_ids.T, combine.T, w_gate[0], w_up[0], w_down[0])
    return (token_grad, gate_g[None], up_g[None], down_g[None])


def fits_kernel(mesh):
    shape = mesh.shape
    return shape["section"] == 2 and shape["expert"] == 4 and shape["tp"] == 4


def solution(mesh):
    return jax.shard_map(
        on_device_kernel if fits_kernel(mesh) else on_device,
        mesh=mesh,
        in_specs=(
            P("expert", ("tp", "section")),
            P("expert", ("tp", "section")),
            P("expert", None),
            P("expert", None),
            P("expert", "tp", "section"),
            P("expert", "tp", "section"),
            P("expert", "section", "tp"),
        ),
        out_specs=(
            P("expert", ("tp", "section")),
            P("expert", "tp", "section"),
            P("expert", "tp", "section"),
            P("expert", "section", "tp"),
        ),
        check_vma=False,
    )
```

```python
import functools

import jax
import jax.numpy as jnp
from jax import lax
from jax.experimental import pallas as pl
from jax.experimental.pallas import tpu as pltpu
from jax.sharding import PartitionSpec as P

MESH = pl.DeviceIdType.MESH


def block_slots(expert_ids, experts, capacity):
    flat_ids = expert_ids.reshape(-1)
    pick_count = flat_ids.shape[0]
    onehot = (flat_ids[:, None] == jnp.arange(experts, dtype=jnp.int32)[None, :]).astype(jnp.int32)
    earlier = jnp.cumsum(onehot, axis=0) - onehot
    slot_index = jnp.sum(earlier * onehot, axis=1)
    place_index = flat_ids * capacity + slot_index
    source = (
        jnp.zeros((experts * capacity,), jnp.int32)
        .at[place_index]
        .set(jnp.arange(pick_count, dtype=jnp.int32))
    )
    filled = (
        jnp.zeros((experts * capacity,), jnp.int32)
        .at[place_index]
        .set(jnp.ones((pick_count,), jnp.int32))
    )
    return (slot_index, source.reshape(experts, capacity), filled.reshape(experts, capacity))


def round_back(values):
    return lax.optimization_barrier(values.astype(jnp.bfloat16)).astype(jnp.float32)


def local_grads(gate_pre, up_pre, hidden_grad):
    sigmoid_g = jax.nn.sigmoid(gate_pre)
    activated = (gate_pre * sigmoid_g * up_pre).astype(jnp.bfloat16)
    gate_grad = (hidden_grad * up_pre * sigmoid_g * (1.0 + gate_pre * (1.0 - sigmoid_g))).astype(
        jnp.bfloat16
    )
    up_grad = (hidden_grad * gate_pre * sigmoid_g).astype(jnp.bfloat16)
    return (activated, gate_grad, up_grad)


def fill_buffers(source, filled, combine, top_count, features, grad_rows):
    tok_count = features.shape[0]
    token_index = source // top_count
    keep_mask = (filled > 0)[:, :, None]
    positions = jnp.arange(tok_count, dtype=jnp.int32)[None, None, :]
    selector = jnp.logical_and(token_index[:, :, None] == positions, keep_mask).astype(jnp.bfloat16)
    rows_in = jnp.einsum(
        "ect,td->ecd", selector, features, preferred_element_type=jnp.float32
    ).astype(jnp.bfloat16)
    picked_grad = jnp.einsum("ect,td->ecd", selector, grad_rows, preferred_element_type=jnp.float32)
    weight = combine.reshape(-1)[source]
    grad_in = (picked_grad * weight[:, :, None]).astype(jnp.bfloat16)
    return (rows_in, grad_in)


def token_picker(pick_rows, tok_dev, top_count, row_count):
    columns = jnp.arange(row_count, dtype=jnp.int32)[None, None, :]
    hits = (pick_rows.reshape(tok_dev, top_count)[:, :, None] == columns).astype(jnp.int32)
    return jnp.sum(hits, axis=1)


def contract_rows(left_side, right_side):
    return lax.dot_general(
        left_side, right_side, (((0,), (0,)), ((), ())), preferred_element_type=jnp.float32
    )


def contract_last(left_side, right_side):
    return lax.dot_general(
        left_side, right_side, (((1,), (1,)), ((), ())), preferred_element_type=jnp.float32
    )


def on_device(tokens, out_grad, expert_ids, combine, w_gate, w_up, w_down):
    tok_dev, top_count = expert_ids.shape
    experts = lax.axis_size("expert")
    capacity = (tok_dev * top_count * 9 + 8 * experts - 1) // (8 * experts)
    slot_index, source, filled = block_slots(expert_ids, experts, capacity)
    features, grad_rows = (
        lax.all_gather(tokens, "section", axis=1, tiled=True),
        lax.all_gather(out_grad, "section", axis=1, tiled=True),
    )
    send_rows, send_grads = fill_buffers(source, filled, combine, top_count, features, grad_rows)
    got_rows, got_grads = (
        lax.all_to_all(send_rows, "expert", split_axis=0, concat_axis=0, tiled=True),
        lax.all_to_all(send_grads, "expert", split_axis=0, concat_axis=0, tiled=True),
    )
    width_dev = got_rows.shape[2]
    rows_in = got_rows.reshape(-1, width_dev)
    grad_in = got_grads.reshape(-1, width_dev)
    gate_w = w_gate[0]
    up_w = w_up[0]
    down_w = w_down[0]
    gate_part = round_back(jnp.dot(rows_in, gate_w, preferred_element_type=jnp.float32))
    up_part = round_back(jnp.dot(rows_in, up_w, preferred_element_type=jnp.float32))
    hidden_part = round_back(contract_last(grad_in, down_w))
    gate_pre, up_pre, hidden_grad = (
        lax.psum(gate_part.astype(jnp.bfloat16), "tp").astype(jnp.float32),
        lax.psum(up_part.astype(jnp.bfloat16), "tp").astype(jnp.float32),
        lax.psum(hidden_part.astype(jnp.bfloat16), "tp").astype(jnp.float32),
    )
    activated, gate_grad, up_grad = local_grads(gate_pre, up_pre, hidden_grad)
    row_float = contract_last(gate_grad, gate_w) + contract_last(up_grad, up_w)
    flat_ids = expert_ids.reshape(-1)
    pick_rows = flat_ids * capacity + slot_index
    picker = token_picker(pick_rows, tok_dev, top_count, experts * capacity)
    row_grad = row_float.astype(jnp.bfloat16)
    returned = lax.all_to_all(
        row_grad.reshape(experts, capacity, width_dev),
        "expert",
        split_axis=0,
        concat_axis=0,
        tiled=True,
    )
    summed = jnp.dot(
        picker.astype(jnp.bfloat16),
        returned.reshape(experts * capacity, width_dev),
        preferred_element_type=jnp.float32,
    )
    token_grad = lax.psum_scatter(
        summed.astype(jnp.bfloat16), "section", scatter_dimension=1, tiled=True
    )
    down_wgrad = contract_rows(activated, grad_in).astype(jnp.bfloat16)[None]
    gate_wgrad = contract_rows(rows_in, gate_grad).astype(jnp.bfloat16)[None]
    up_wgrad = contract_rows(rows_in, up_grad).astype(jnp.bfloat16)[None]
    return (token_grad, gate_wgrad, up_wgrad, down_wgrad)


def expert_kernel(
    n,
    slots,
    tok_hbm,
    grad_hbm,
    ids_ref,
    combine_ref,
    gate_hbm,
    up_hbm,
    down_hbm,
    token_out,
    gate_out,
    up_out,
    down_out,
    tok_ref,
    grad_ref,
    both_w,
    down_w,
    both_t,
    down_t,
    both_acc,
    down_acc,
    picks,
    send_rows,
    send_grads,
    rows,
    grads,
    parts,
    got_parts,
    local,
    halves,
    got_half,
    back,
    returned,
    gate_g,
    up_g,
    down_g,
    io_sem,
    z_send,
    z_recv,
    s_send,
    s_recv,
    p_send,
    p_recv,
    a_send,
    a_recv,
    h_send,
    h_recv,
    r_send,
    r_recv,
):
    sec = lax.axis_index("section")
    exp = lax.axis_index("expert")
    tp = lax.axis_index("tp")
    other = 1 - sec
    tok_dev, width = tok_ref.shape
    hidden = down_w.shape[0]
    groups = hidden // 128
    share = parts.shape[1] // n
    sign = 2 * lax.rem(exp, 2) - 1

    def hop(axis, index):
        place = {"section": sec, "expert": exp, "tp": tp}
        place[axis] = index
        return (place["section"], place["expert"], place["tp"])

    def remote(src, dst, send, recv, target):
        return pltpu.make_async_remote_copy(
            src_ref=src,
            dst_ref=dst,
            send_sem=send,
            recv_sem=recv,
            device_id=target,
            device_id_type=MESH,
        )

    def partner(k):
        return lax.rem(exp + n + sign * k, n)

    fetch = [
        pltpu.make_async_copy(tok_hbm, tok_ref, io_sem.at[0]),
        pltpu.make_async_copy(grad_hbm, grad_ref, io_sem.at[1]),
    ]
    loads = [pltpu.make_async_copy(down_hbm, down_w, io_sem.at[2])]
    for j in range(groups):
        for index, source in enumerate((gate_hbm, up_hbm)):
            loads.append(
                pltpu.make_async_copy(
                    source.at[:, pl.ds(j * 128, 128)],
                    both_w.at[:, pl.ds((2 * j + index) * 128, 128)],
                    io_sem.at[3 + 2 * j + index],
                )
            )
    for copy in fetch + loads:
        copy.start()

    barrier = pltpu.get_barrier_semaphore()
    pl.semaphore_signal(barrier, inc=1, device_id=hop("section", other), device_id_type=MESH)
    for k in range(1, n):
        pl.semaphore_signal(barrier, inc=1, device_id=hop("expert", partner(k)), device_id_type=MESH)
        pl.semaphore_signal(
            barrier, inc=1, device_id=hop("tp", lax.rem(tp + k, n)), device_id_type=MESH
        )

    target = lax.rem(exp + 2 * n + sign * lax.rem(lax.broadcasted_iota(jnp.int32, (8, tok_dev), 0), n), n)
    first = ids_ref[0:1, :] == target
    second = ids_ref[1:2, :] == target
    named = jnp.logical_or(first, second).astype(jnp.float32)
    weight = jnp.where(first, combine_ref[0:1, :], 0.0) + jnp.where(second, combine_ref[1:2, :], 0.0)
    earlier = (
        lax.broadcasted_iota(jnp.int32, (tok_dev, tok_dev), 0)
        < lax.broadcasted_iota(jnp.int32, (tok_dev, tok_dev), 1)
    ).astype(jnp.bfloat16)
    slot = jnp.dot(named.astype(jnp.bfloat16), earlier, preferred_element_type=jnp.float32)
    place = jnp.where(named > 0.0, slot, -1.0)
    numbers = lax.broadcasted_iota(jnp.int32, (slots, tok_dev), 0).astype(jnp.float32)
    spare = n * share - groups * slots
    if spare > 0:
        for k in range(n):
            parts[k, groups * slots :, :] = jnp.zeros((spare, 384), jnp.bfloat16)

    def block(k):
        return pl.ds(k * slots, slots)

    def z_copies(k):
        goal = hop("expert", partner(k))
        return (
            remote(send_rows.at[k - 1], rows.at[sec, block(k)], z_send.at[0, k - 1], z_recv.at[0, k - 1], goal),
            remote(send_grads.at[k - 1], grads.at[sec, block(k)], z_send.at[1, k - 1], z_recv.at[1, k - 1], goal),
        )

    def s_copies(k):
        goal = hop("section", other)
        return (
            remote(rows.at[sec, block(k)], rows.at[sec, block(k)], s_send.at[0, k], s_recv.at[0, k], goal),
            remote(grads.at[sec, block(k)], grads.at[sec, block(k)], s_send.at[1, k], s_recv.at[1, k], goal),
        )

    def p_copy(k, r):
        goal = lax.rem(tp + r, n)
        span = pl.ds(pl.multiple_of(goal * share, share), share)
        return remote(
            parts.at[k, span], got_parts.at[k, r - 1], p_send.at[k, r - 1], p_recv.at[k, r - 1], hop("tp", goal)
        )

    mine = pl.ds(pl.multiple_of(tp * share, share), share)

    def a_copy(k, r):
        return remote(
            local.at[k, mine], local.at[k, mine], a_send.at[k, r - 1], a_recv.at[k, r - 1], hop("tp", lax.rem(tp + r, n))
        )

    def h_copy(k):
        return remote(halves.at[k], got_half.at[k], h_send.at[k], h_recv.at[k], hop("section", other))

    def r_copy(k):
        return remote(back.at[k - 1], returned.at[k], r_send.at[k - 1], r_recv.at[k - 1], hop("expert", partner(k)))

    far_first = (2, 1, 3)

    for copy in fetch:
        copy.wait()
    for turn, k in enumerate((1, 2, 0, 3)):
        pick = (place[k : k + 1, :] == numbers).astype(jnp.float32)
        spread = jnp.sum(pick * weight[k : k + 1, :], axis=1, keepdims=True)
        pick = pick.astype(jnp.bfloat16)
        picks[k] = pick
        picked = jnp.dot(pick, tok_ref[...], preferred_element_type=jnp.float32).astype(jnp.bfloat16)
        if k == 0:
            rows[sec, block(0)] = picked
        else:
            send_rows[k - 1] = picked
            if turn == 0:
                pl.semaphore_wait(barrier, 2 * n - 1)
            z_copies(k)[0].start()
        picked_grad = jnp.dot(pick, grad_ref[...], preferred_element_type=jnp.float32)
        picked_grad = (picked_grad * spread).astype(jnp.bfloat16)
        if k == 0:
            grads[sec, block(0)] = picked_grad
            for copy in s_copies(0):
                copy.start()
        else:
            send_grads[k - 1] = picked_grad
            z_copies(k)[1].start()

    for load in loads:
        load.wait()
    for low in range(0, 2 * width, 256):
        both_t[:, low : low + 256] = both_w[low : low + 256, :].T
        down_t[low : low + 256, :] = down_w[:, low : low + 256].T

    def arrive(k):
        for copy, onward in zip(z_copies(k), s_copies(k)):
            copy.wait_recv()
            onward.start()

    def forward(k):
        for copy in s_copies(k):
            copy.wait_recv()
        pre = jnp.dot(rows[0, block(k)], both_w[0:width, :], preferred_element_type=jnp.float32)
        pre += jnp.dot(rows[1, block(k)], both_w[width : 2 * width, :], preferred_element_type=jnp.float32)
        inner = jnp.dot(grads[0, block(k)], down_t[0:width, :], preferred_element_type=jnp.float32)
        inner += jnp.dot(grads[1, block(k)], down_t[width : 2 * width, :], preferred_element_type=jnp.float32)
        for j in range(groups):
            parts[k, j * slots : (j + 1) * slots, 0:256] = pre[:, j * 256 : (j + 1) * 256].astype(jnp.bfloat16)
            parts[k, j * slots : (j + 1) * slots, 256:384] = inner[:, j * 128 : (j + 1) * 128].astype(jnp.bfloat16)
        for r in far_first:
            p_copy(k, r).start()

    def reduce_local(k):
        summed = parts[k, mine, :].astype(jnp.float32)
        for r in range(1, n):
            p_copy(k, r).wait_recv()
            summed += got_parts[k, r - 1].astype(jnp.float32)
        activated, gate_grad, up_grad = local_grads(summed[:, 0:128], summed[:, 128:256], summed[:, 256:384])
        local[k, mine, 0:128] = gate_grad
        local[k, mine, 128:256] = up_grad
        local[k, mine, 256:384] = activated
        for r in far_first:
            a_copy(k, r).start()

    def row_side(k, side):
        span = pl.ds(pl.multiple_of(side * width, width), width)
        return jnp.dot(gate_up(k), both_t[:, span], preferred_element_type=jnp.float32)

    def gate_up(k):
        return jnp.concatenate(
            [local[k, j * slots : (j + 1) * slots, 0:256] for j in range(groups)], axis=1
        )

    def active(k):
        return jnp.concatenate(
            [local[k, j * slots : (j + 1) * slots, 256:384] for j in range(groups)], axis=1
        )

    def backward(k):
        for r in range(1, n):
            a_copy(k, r).wait_recv()
        halves[k] = row_side(k, other).astype(jnp.bfloat16)
        h_copy(k).start()

    def give_back(k):
        own = row_side(k, sec)
        h_copy(k).wait_recv()
        whole = (own + got_half[k].astype(jnp.float32)).astype(jnp.bfloat16)
        if k == 0:
            returned[0] = whole
        else:
            back[k - 1] = whole
            r_copy(k).start()

    chunk = 256
    pieces = [(side, low) for side in range(2) for low in range(0, width, chunk)]

    def both_piece(side, low, blocks):
        return sum(contract_rows(rows[side, block(k), low : low + chunk], gate_up(k)) for k in blocks)

    def down_piece(side, low, blocks):
        return sum(contract_rows(active(k), grads[side, block(k), low : low + chunk]) for k in blocks)

    forward(0)
    arrive(1)
    reduce_local(0)
    forward(1)
    backward(0)
    arrive(3)
    reduce_local(1)
    forward(3)
    give_back(0)
    backward(1)
    arrive(2)
    give_back(1)
    forward(2)
    reduce_local(3)
    backward(3)
    give_back(3)
    early = (0, 1, 3)
    for side, low in pieces:
        start = side * width + low
        both_acc[start : start + chunk, :] = both_piece(side, low, early)
    reduce_local(2)
    for side, low in pieces:
        start = side * width + low
        down_acc[:, start : start + chunk] = down_piece(side, low, early)
    backward(2)
    give_back(2)
    for side, low in pieces:
        start = side * width + low
        total = (both_acc[start : start + chunk, :] + both_piece(side, low, (2,))).astype(jnp.bfloat16)
        for j in range(groups):
            gate_g[start : start + chunk, j * 128 : (j + 1) * 128] = total[:, j * 256 : j * 256 + 128]
            up_g[start : start + chunk, j * 128 : (j + 1) * 128] = total[:, j * 256 + 128 : (j + 1) * 256]
    stores = [
        pltpu.make_async_copy(gate_g, gate_out, io_sem.at[0]),
        pltpu.make_async_copy(up_g, up_out, io_sem.at[1]),
        pltpu.make_async_copy(down_g, down_out, io_sem.at[2]),
    ]
    stores[0].start()
    stores[1].start()
    for side, low in pieces:
        start = side * width + low
        down_g[:, start : start + chunk] = (
            down_acc[:, start : start + chunk] + down_piece(side, low, (2,))
        ).astype(jnp.bfloat16)
    stores[2].start()

    total = contract_rows(picks[0], returned[0])
    for k in (1, 3, 2):
        r_copy(k).wait_recv()
        total += contract_rows(picks[k], returned[k])
    token_out[...] = total.astype(jnp.bfloat16)

    for k in range(n):
        for copy in s_copies(k):
            copy.wait_send()
        h_copy(k).wait_send()
        for r in range(1, n):
            p_copy(k, r).wait_send()
            a_copy(k, r).wait_send()
        if k > 0:
            for copy in z_copies(k):
                copy.wait_send()
            r_copy(k).wait_send()
    for store in stores:
        store.wait()


def hand_over(*refs):
    count = (len(refs) - 1) // 2
    copies = [
        pltpu.make_async_copy(refs[index], refs[count + index], refs[-1].at[index]) for index in range(count)
    ]
    for copy in copies:
        copy.start()
    for copy in copies:
        copy.wait()


def on_device_kernel(tokens, out_grad, expert_ids, combine, w_gate, w_up, w_down):
    tok_dev, top_count = expert_ids.shape
    n = lax.axis_size("expert")
    capacity = (tok_dev * top_count * 9 + 8 * n - 1) // (8 * n)
    slots = (capacity + 15) // 16 * 16
    width = tokens.shape[1]
    depth, hidden = w_gate.shape[1:]
    groups = hidden // 128
    share = (groups * slots + 16 * n - 1) // (16 * n) * 16
    bf16 = jnp.bfloat16
    vmem = pl.BlockSpec(memory_space=pltpu.VMEM)
    hbm = pl.BlockSpec(memory_space=pl.ANY)
    dma = pltpu.SemaphoreType.DMA
    results = pl.pallas_call(
        functools.partial(expert_kernel, n, slots),
        out_shape=(
            jax.ShapeDtypeStruct((tok_dev, width), bf16),
            jax.ShapeDtypeStruct((depth, hidden), bf16),
            jax.ShapeDtypeStruct((depth, hidden), bf16),
            jax.ShapeDtypeStruct((hidden, depth), bf16),
        ),
        in_specs=[hbm, hbm, vmem, vmem, hbm, hbm, hbm],
        out_specs=(vmem, hbm, hbm, hbm),
        scratch_shapes=[
            pltpu.VMEM((tok_dev, width), bf16),
            pltpu.VMEM((tok_dev, width), bf16),
            pltpu.VMEM((depth, 2 * hidden), bf16),
            pltpu.VMEM((hidden, depth), bf16),
            pltpu.VMEM((2 * hidden, depth), bf16),
            pltpu.VMEM((depth, hidden), bf16),
            pltpu.VMEM((depth, 2 * hidden), jnp.float32),
            pltpu.VMEM((hidden, depth), jnp.float32),
            pltpu.VMEM((n, slots, tok_dev), bf16),
            pltpu.VMEM((n - 1, slots, width), bf16),
            pltpu.VMEM((n - 1, slots, width), bf16),
            pltpu.VMEM((2, n * slots, width), bf16),
            pltpu.VMEM((2, n * slots, width), bf16),
            pltpu.VMEM((n, n * share, 384), bf16),
            pltpu.VMEM((n, n - 1, share, 384), bf16),
            pltpu.VMEM((n, n * share, 384), bf16),
            pltpu.VMEM((n, slots, width), bf16),
            pltpu.VMEM((n, slots, width), bf16),
            pltpu.VMEM((n - 1, slots, width), bf16),
            pltpu.VMEM((n, slots, width), bf16),
            pltpu.VMEM((depth, hidden), bf16),
            pltpu.VMEM((depth, hidden), bf16),
            pltpu.VMEM((hidden, depth), bf16),
            dma((3 + 2 * groups,)),
            dma((2, n - 1)),
            dma((2, n - 1)),
            dma((2, n)),
            dma((2, n)),
            dma((n, n - 1)),
            dma((n, n - 1)),
            dma((n, n - 1)),
            dma((n, n - 1)),
            dma((n,)),
            dma((n,)),
            dma((n - 1,)),
            dma((n - 1,)),
        ],
        compiler_params=pltpu.CompilerParams(
            collective_id=0, has_side_effects=True, vmem_limit_bytes=63 * 1024 * 1024
        ),
    )(tokens, out_grad, expert_ids.T, combine.T, w_gate[0], w_up[0], w_down[0])
    token_grad, gate_g, up_g, down_g = pl.pallas_call(
        hand_over,
        out_shape=tuple(jax.ShapeDtypeStruct(result.shape, result.dtype) for result in results),
        in_specs=[hbm] * 4,
        out_specs=(hbm,) * 4,
        scratch_shapes=[dma((4,))],
        compiler_params=pltpu.CompilerParams(vmem_limit_bytes=63 * 1024 * 1024),
    )(*results)
    return (token_grad, gate_g[None], up_g[None], down_g[None])


def fits_kernel(mesh):
    shape = mesh.shape
    return shape["section"] == 2 and shape["expert"] == 4 and shape["tp"] == 4


def solution(mesh):
    return jax.shard_map(
        on_device_kernel if fits_kernel(mesh) else on_device,
        mesh=mesh,
        in_specs=(
            P("expert", ("tp", "section")),
            P("expert", ("tp", "section")),
            P("expert", None),
            P("expert", None),
            P("expert", "tp", "section"),
            P("expert", "tp", "section"),
            P("expert", "section", "tp"),
        ),
        out_specs=(
            P("expert", ("tp", "section")),
            P("expert", "tp", "section"),
            P("expert", "tp", "section"),
            P("expert", "section", "tp"),
        ),
        check_vma=False,
    )
```

```python
import functools

import jax
import jax.numpy as jnp
from jax import lax
from jax.experimental import pallas as pl
from jax.experimental.pallas import tpu as pltpu
from jax.sharding import PartitionSpec as P

MESH = pl.DeviceIdType.MESH


def block_slots(expert_ids, experts, capacity):
    flat_ids = expert_ids.reshape(-1)
    pick_count = flat_ids.shape[0]
    onehot = (flat_ids[:, None] == jnp.arange(experts, dtype=jnp.int32)[None, :]).astype(jnp.int32)
    earlier = jnp.cumsum(onehot, axis=0) - onehot
    slot_index = jnp.sum(earlier * onehot, axis=1)
    place_index = flat_ids * capacity + slot_index
    source = (
        jnp.zeros((experts * capacity,), jnp.int32)
        .at[place_index]
        .set(jnp.arange(pick_count, dtype=jnp.int32))
    )
    filled = (
        jnp.zeros((experts * capacity,), jnp.int32)
        .at[place_index]
        .set(jnp.ones((pick_count,), jnp.int32))
    )
    return (slot_index, source.reshape(experts, capacity), filled.reshape(experts, capacity))


def round_back(values):
    return lax.optimization_barrier(values.astype(jnp.bfloat16)).astype(jnp.float32)


def local_grads(gate_pre, up_pre, hidden_grad):
    sigmoid_g = jax.nn.sigmoid(gate_pre)
    activated = (gate_pre * sigmoid_g * up_pre).astype(jnp.bfloat16)
    gate_grad = (hidden_grad * up_pre * sigmoid_g * (1.0 + gate_pre * (1.0 - sigmoid_g))).astype(
        jnp.bfloat16
    )
    up_grad = (hidden_grad * gate_pre * sigmoid_g).astype(jnp.bfloat16)
    return (activated, gate_grad, up_grad)


def fill_buffers(source, filled, combine, top_count, features, grad_rows):
    tok_count = features.shape[0]
    token_index = source // top_count
    keep_mask = (filled > 0)[:, :, None]
    positions = jnp.arange(tok_count, dtype=jnp.int32)[None, None, :]
    selector = jnp.logical_and(token_index[:, :, None] == positions, keep_mask).astype(jnp.bfloat16)
    rows_in = jnp.einsum(
        "ect,td->ecd", selector, features, preferred_element_type=jnp.float32
    ).astype(jnp.bfloat16)
    picked_grad = jnp.einsum("ect,td->ecd", selector, grad_rows, preferred_element_type=jnp.float32)
    weight = combine.reshape(-1)[source]
    grad_in = (picked_grad * weight[:, :, None]).astype(jnp.bfloat16)
    return (rows_in, grad_in)


def token_picker(pick_rows, tok_dev, top_count, row_count):
    columns = jnp.arange(row_count, dtype=jnp.int32)[None, None, :]
    hits = (pick_rows.reshape(tok_dev, top_count)[:, :, None] == columns).astype(jnp.int32)
    return jnp.sum(hits, axis=1)


def contract_rows(left_side, right_side):
    return lax.dot_general(
        left_side, right_side, (((0,), (0,)), ((), ())), preferred_element_type=jnp.float32
    )


def contract_last(left_side, right_side):
    return lax.dot_general(
        left_side, right_side, (((1,), (1,)), ((), ())), preferred_element_type=jnp.float32
    )


def on_device(tokens, out_grad, expert_ids, combine, w_gate, w_up, w_down):
    tok_dev, top_count = expert_ids.shape
    experts = lax.axis_size("expert")
    capacity = (tok_dev * top_count * 9 + 8 * experts - 1) // (8 * experts)
    slot_index, source, filled = block_slots(expert_ids, experts, capacity)
    features, grad_rows = (
        lax.all_gather(tokens, "section", axis=1, tiled=True),
        lax.all_gather(out_grad, "section", axis=1, tiled=True),
    )
    send_rows, send_grads = fill_buffers(source, filled, combine, top_count, features, grad_rows)
    got_rows, got_grads = (
        lax.all_to_all(send_rows, "expert", split_axis=0, concat_axis=0, tiled=True),
        lax.all_to_all(send_grads, "expert", split_axis=0, concat_axis=0, tiled=True),
    )
    width_dev = got_rows.shape[2]
    rows_in = got_rows.reshape(-1, width_dev)
    grad_in = got_grads.reshape(-1, width_dev)
    gate_w = w_gate[0]
    up_w = w_up[0]
    down_w = w_down[0]
    gate_part = round_back(jnp.dot(rows_in, gate_w, preferred_element_type=jnp.float32))
    up_part = round_back(jnp.dot(rows_in, up_w, preferred_element_type=jnp.float32))
    hidden_part = round_back(contract_last(grad_in, down_w))
    gate_pre, up_pre, hidden_grad = (
        lax.psum(gate_part.astype(jnp.bfloat16), "tp").astype(jnp.float32),
        lax.psum(up_part.astype(jnp.bfloat16), "tp").astype(jnp.float32),
        lax.psum(hidden_part.astype(jnp.bfloat16), "tp").astype(jnp.float32),
    )
    activated, gate_grad, up_grad = local_grads(gate_pre, up_pre, hidden_grad)
    row_float = contract_last(gate_grad, gate_w) + contract_last(up_grad, up_w)
    flat_ids = expert_ids.reshape(-1)
    pick_rows = flat_ids * capacity + slot_index
    picker = token_picker(pick_rows, tok_dev, top_count, experts * capacity)
    row_grad = row_float.astype(jnp.bfloat16)
    returned = lax.all_to_all(
        row_grad.reshape(experts, capacity, width_dev),
        "expert",
        split_axis=0,
        concat_axis=0,
        tiled=True,
    )
    summed = jnp.dot(
        picker.astype(jnp.bfloat16),
        returned.reshape(experts * capacity, width_dev),
        preferred_element_type=jnp.float32,
    )
    token_grad = lax.psum_scatter(
        summed.astype(jnp.bfloat16), "section", scatter_dimension=1, tiled=True
    )
    down_wgrad = contract_rows(activated, grad_in).astype(jnp.bfloat16)[None]
    gate_wgrad = contract_rows(rows_in, gate_grad).astype(jnp.bfloat16)[None]
    up_wgrad = contract_rows(rows_in, up_grad).astype(jnp.bfloat16)[None]
    return (token_grad, gate_wgrad, up_wgrad, down_wgrad)


def expert_kernel(
    n,
    slots,
    tok_hbm,
    grad_hbm,
    ids_ref,
    combine_ref,
    gate_hbm,
    up_hbm,
    down_hbm,
    token_out,
    gate_out,
    up_out,
    down_out,
    tok_ref,
    grad_ref,
    both_w,
    down_w,
    both_t,
    down_t,
    place_ref,
    weight_ref,
    picks,
    send_rows,
    send_grads,
    rows,
    grads,
    parts,
    got_parts,
    local,
    halves,
    got_half,
    back,
    returned,
    gate_g,
    up_g,
    down_g,
    io_sem,
    z_send,
    z_recv,
    s_send,
    s_recv,
    p_send,
    p_recv,
    a_send,
    a_recv,
    h_send,
    h_recv,
    r_send,
    r_recv,
):
    sec = lax.axis_index("section")
    exp = lax.axis_index("expert")
    tp = lax.axis_index("tp")
    other = 1 - sec
    tok_dev, width = tok_ref.shape
    hidden = down_w.shape[0]
    groups = hidden // 128
    share = parts.shape[1] // n
    sign = 2 * lax.rem(exp, 2) - 1

    def hop(axis, index):
        place = {"section": sec, "expert": exp, "tp": tp}
        place[axis] = index
        return (place["section"], place["expert"], place["tp"])

    def remote(src, dst, send, recv, target):
        return pltpu.make_async_remote_copy(
            src_ref=src,
            dst_ref=dst,
            send_sem=send,
            recv_sem=recv,
            device_id=target,
            device_id_type=MESH,
        )

    def partner(k):
        return lax.rem(exp + n + sign * k, n)

    fetch = [
        pltpu.make_async_copy(tok_hbm, tok_ref, io_sem.at[0]),
        pltpu.make_async_copy(grad_hbm, grad_ref, io_sem.at[1]),
    ]
    loads = [pltpu.make_async_copy(down_hbm, down_w, io_sem.at[2])]
    for j in range(groups):
        for index, source in enumerate((gate_hbm, up_hbm)):
            loads.append(
                pltpu.make_async_copy(
                    source.at[:, pl.ds(j * 128, 128)],
                    both_w.at[:, pl.ds((2 * j + index) * 128, 128)],
                    io_sem.at[3 + 2 * j + index],
                )
            )
    for copy in fetch + loads:
        copy.start()

    barrier = pltpu.get_barrier_semaphore()
    pl.semaphore_signal(barrier, inc=1, device_id=hop("section", other), device_id_type=MESH)
    for k in range(1, n):
        pl.semaphore_signal(barrier, inc=1, device_id=hop("expert", partner(k)), device_id_type=MESH)
        pl.semaphore_signal(
            barrier, inc=1, device_id=hop("tp", lax.rem(tp + k, n)), device_id_type=MESH
        )

    target = lax.rem(exp + 2 * n + sign * lax.rem(lax.broadcasted_iota(jnp.int32, (8, tok_dev), 0), n), n)
    first = ids_ref[0:1, :] == target
    second = ids_ref[1:2, :] == target
    named = jnp.logical_or(first, second).astype(jnp.float32)
    weight = jnp.where(first, combine_ref[0:1, :], 0.0) + jnp.where(second, combine_ref[1:2, :], 0.0)
    earlier = (
        lax.broadcasted_iota(jnp.int32, (tok_dev, tok_dev), 0)
        < lax.broadcasted_iota(jnp.int32, (tok_dev, tok_dev), 1)
    ).astype(jnp.bfloat16)
    slot = jnp.dot(named.astype(jnp.bfloat16), earlier, preferred_element_type=jnp.float32)
    place = jnp.where(named > 0.0, slot, -1.0)
    numbers = lax.broadcasted_iota(jnp.int32, (slots, tok_dev), 0).astype(jnp.float32)
    spare = n * share - groups * slots
    if spare > 0:
        for k in range(n):
            parts[k, groups * slots :, :] = jnp.zeros((spare, 384), jnp.bfloat16)

    def block(k):
        return pl.ds(pl.multiple_of(k * slots, 16), slots)

    def z_copies(k):
        goal = hop("expert", partner(k))
        return (
            remote(send_rows.at[k - 1], rows.at[sec, block(k)], z_send.at[0, k - 1], z_recv.at[0, k - 1], goal),
            remote(send_grads.at[k - 1], grads.at[sec, block(k)], z_send.at[1, k - 1], z_recv.at[1, k - 1], goal),
        )

    def s_copies(k):
        goal = hop("section", other)
        return (
            remote(rows.at[sec, block(k)], rows.at[sec, block(k)], s_send.at[0, k], s_recv.at[0, k], goal),
            remote(grads.at[sec, block(k)], grads.at[sec, block(k)], s_send.at[1, k], s_recv.at[1, k], goal),
        )

    def p_copy(k, r):
        goal = lax.rem(tp + r, n)
        span = pl.ds(pl.multiple_of(goal * share, share), share)
        return remote(
            parts.at[k, span], got_parts.at[k, r - 1], p_send.at[k, r - 1], p_recv.at[k, r - 1], hop("tp", goal)
        )

    mine = pl.ds(pl.multiple_of(tp * share, share), share)

    def a_copy(k, r):
        return remote(
            local.at[k, mine], local.at[k, mine], a_send.at[k, r - 1], a_recv.at[k, r - 1], hop("tp", lax.rem(tp + r, n))
        )

    def h_copy(k):
        return remote(halves.at[k], got_half.at[k], h_send.at[k], h_recv.at[k], hop("section", other))

    def r_copy(k):
        return remote(back.at[k - 1], returned.at[k], r_send.at[k - 1], r_recv.at[k - 1], hop("expert", partner(k)))

    far_first = (2, 1, 3)

    for copy in fetch:
        copy.wait()
    place_ref[...] = place
    weight_ref[...] = weight
    pl.semaphore_wait(barrier, 2 * n - 1)

    @pl.loop(1, n + 1)
    def _(turn):
        k = lax.rem(turn, n)
        pick = (place_ref[pl.ds(k, 1), :] == numbers).astype(jnp.float32)
        spread = jnp.sum(pick * weight_ref[pl.ds(k, 1), :], axis=1, keepdims=True)
        pick = pick.astype(jnp.bfloat16)
        picks[k] = pick
        picked = jnp.dot(pick, tok_ref[...], preferred_element_type=jnp.float32).astype(jnp.bfloat16)
        picked_grad = jnp.dot(pick, grad_ref[...], preferred_element_type=jnp.float32)
        picked_grad = (picked_grad * spread).astype(jnp.bfloat16)

        @pl.when(k == 0)
        def _():
            rows[sec, block(0)] = picked
            grads[sec, block(0)] = picked_grad
            for copy in s_copies(0):
                copy.start()

        @pl.when(k != 0)
        def _():
            send_rows[k - 1] = picked
            send_grads[k - 1] = picked_grad
            for copy in z_copies(k):
                copy.start()

    for load in loads:
        load.wait()

    @pl.loop(0, 2 * width // 256)
    def _(index):
        span = pl.ds(pl.multiple_of(index * 256, 256), 256)
        both_t[:, span] = both_w[span, :].T
        down_t[span, :] = down_w[:, span].T


    def arrive(k):
        for copy, onward in zip(z_copies(k), s_copies(k)):
            copy.wait_recv()
            onward.start()

    def forward(k):
        for copy in s_copies(k):
            copy.wait_recv()
        pre = jnp.dot(rows[0, block(k)], both_w[0:width, :], preferred_element_type=jnp.float32)
        pre += jnp.dot(rows[1, block(k)], both_w[width : 2 * width, :], preferred_element_type=jnp.float32)
        inner = jnp.dot(grads[0, block(k)], down_t[0:width, :], preferred_element_type=jnp.float32)
        inner += jnp.dot(grads[1, block(k)], down_t[width : 2 * width, :], preferred_element_type=jnp.float32)
        for j in range(groups):
            parts[k, j * slots : (j + 1) * slots, 0:256] = pre[:, j * 256 : (j + 1) * 256].astype(jnp.bfloat16)
            parts[k, j * slots : (j + 1) * slots, 256:384] = inner[:, j * 128 : (j + 1) * 128].astype(jnp.bfloat16)
        for r in far_first:
            p_copy(k, r).start()

    def reduce_local(k):
        summed = parts[k, mine, :].astype(jnp.float32)
        for r in range(1, n):
            p_copy(k, r).wait_recv()
            summed += got_parts[k, r - 1].astype(jnp.float32)
        activated, gate_grad, up_grad = local_grads(summed[:, 0:128], summed[:, 128:256], summed[:, 256:384])
        local[k, mine, 0:128] = gate_grad
        local[k, mine, 128:256] = up_grad
        local[k, mine, 256:384] = activated
        for r in far_first:
            a_copy(k, r).start()

    def row_side(k, side):
        span = pl.ds(pl.multiple_of(side * width, width), width)
        return jnp.dot(gate_up(k), both_t[:, span], preferred_element_type=jnp.float32)

    def gate_up(k):
        return jnp.concatenate(
            [local[k, j * slots : (j + 1) * slots, 0:256] for j in range(groups)], axis=1
        )

    def active(k):
        return jnp.concatenate(
            [local[k, j * slots : (j + 1) * slots, 256:384] for j in range(groups)], axis=1
        )

    def backward(k):
        for r in range(1, n):
            a_copy(k, r).wait_recv()
        halves[k] = row_side(k, other).astype(jnp.bfloat16)
        h_copy(k).start()

    def give_back(k):
        own = row_side(k, sec)
        h_copy(k).wait_recv()
        whole = (own + got_half[k].astype(jnp.float32)).astype(jnp.bfloat16)

        @pl.when(k == 0)
        def _():
            returned[0] = whole

        @pl.when(k != 0)
        def _():
            back[k - 1] = whole
            r_copy(k).start()


    def nth(turn):
        return jnp.where(turn < 2, turn, n + 1 - turn)

    @pl.loop(0, n + 2)
    def _(turn):
        @pl.when(jnp.logical_and(turn > 0, turn < n))
        def _():
            arrive(nth(turn))

        @pl.when(jnp.logical_and(turn > 0, turn <= n))
        def _():
            reduce_local(nth(turn - 1))

        @pl.when(turn < n)
        def _():
            forward(nth(turn))

        @pl.when(turn > 1)
        def _():
            give_back(nth(turn - 2))

        @pl.when(jnp.logical_and(turn > 0, turn <= n))
        def _():
            backward(nth(turn - 1))

    chunk = 256

    @pl.loop(0, 2 * width // chunk)
    def _(piece):
        per_side = width // chunk
        side = piece // per_side
        low = pl.ds(pl.multiple_of(lax.rem(piece, per_side) * chunk, chunk), chunk)
        span = pl.ds(pl.multiple_of(piece * chunk, chunk), chunk)
        total = sum(
            contract_rows(rows[side, block(k), low], gate_up(k)) for k in range(n)
        ).astype(jnp.bfloat16)
        for j in range(groups):
            gate_g[span, j * 128 : (j + 1) * 128] = total[:, j * 256 : j * 256 + 128]
            up_g[span, j * 128 : (j + 1) * 128] = total[:, j * 256 + 128 : (j + 1) * 256]
        down_g[:, span] = sum(
            contract_rows(active(k), grads[side, block(k), low]) for k in range(n)
        ).astype(jnp.bfloat16)

    stores = [
        pltpu.make_async_copy(gate_g, gate_out, io_sem.at[0]),
        pltpu.make_async_copy(up_g, up_out, io_sem.at[1]),
        pltpu.make_async_copy(down_g, down_out, io_sem.at[2]),
    ]
    for store in stores:
        store.start()

    total = contract_rows(picks[0], returned[0])
    for k in (1, 3, 2):
        r_copy(k).wait_recv()
        total += contract_rows(picks[k], returned[k])
    token_out[...] = total.astype(jnp.bfloat16)

    for k in range(n):
        for copy in s_copies(k):
            copy.wait_send()
        h_copy(k).wait_send()
        for r in range(1, n):
            p_copy(k, r).wait_send()
            a_copy(k, r).wait_send()
        if k > 0:
            for copy in z_copies(k):
                copy.wait_send()
            r_copy(k).wait_send()
    for store in stores:
        store.wait()


def hand_over(count, *refs):
    sources, results, held = refs[:count], refs[count : 2 * count], refs[2 * count : 3 * count]
    load_sem, store_sem = refs[3 * count :]
    loads = [pltpu.make_async_copy(sources[i], held[i], load_sem.at[i]) for i in range(count)]
    stores = [pltpu.make_async_copy(held[i], results[i], store_sem.at[i]) for i in range(count)]
    for load in loads:
        load.start()
    for load, store in zip(loads, stores):
        load.wait()
        store.start()
    for store in stores:
        store.wait()


def on_device_kernel(tokens, out_grad, expert_ids, combine, w_gate, w_up, w_down):
    tok_dev, top_count = expert_ids.shape
    n = lax.axis_size("expert")
    capacity = (tok_dev * top_count * 9 + 8 * n - 1) // (8 * n)
    slots = (capacity + 15) // 16 * 16
    width = tokens.shape[1]
    depth, hidden = w_gate.shape[1:]
    groups = hidden // 128
    share = (groups * slots + 16 * n - 1) // (16 * n) * 16
    bf16 = jnp.bfloat16
    vmem = pl.BlockSpec(memory_space=pltpu.VMEM)
    hbm = pl.BlockSpec(memory_space=pl.ANY)
    dma = pltpu.SemaphoreType.DMA
    results = pl.pallas_call(
        functools.partial(expert_kernel, n, slots),
        out_shape=(
            jax.ShapeDtypeStruct((tok_dev, width), bf16),
            jax.ShapeDtypeStruct((depth, hidden), bf16),
            jax.ShapeDtypeStruct((depth, hidden), bf16),
            jax.ShapeDtypeStruct((hidden, depth), bf16),
        ),
        in_specs=[hbm, hbm, vmem, vmem, hbm, hbm, hbm],
        out_specs=(vmem, hbm, hbm, hbm),
        scratch_shapes=[
            pltpu.VMEM((tok_dev, width), bf16),
            pltpu.VMEM((tok_dev, width), bf16),
            pltpu.VMEM((depth, 2 * hidden), bf16),
            pltpu.VMEM((hidden, depth), bf16),
            pltpu.VMEM((2 * hidden, depth), bf16),
            pltpu.VMEM((depth, hidden), bf16),
            pltpu.VMEM((8, tok_dev), jnp.float32),
            pltpu.VMEM((8, tok_dev), jnp.float32),
            pltpu.VMEM((n, slots, tok_dev), bf16),
            pltpu.VMEM((n - 1, slots, width), bf16),
            pltpu.VMEM((n - 1, slots, width), bf16),
            pltpu.VMEM((2, n * slots, width), bf16),
            pltpu.VMEM((2, n * slots, width), bf16),
            pltpu.VMEM((n, n * share, 384), bf16),
            pltpu.VMEM((n, n - 1, share, 384), bf16),
            pltpu.VMEM((n, n * share, 384), bf16),
            pltpu.VMEM((n, slots, width), bf16),
            pltpu.VMEM((n, slots, width), bf16),
            pltpu.VMEM((n - 1, slots, width), bf16),
            pltpu.VMEM((n, slots, width), bf16),
            pltpu.VMEM((depth, hidden), bf16),
            pltpu.VMEM((depth, hidden), bf16),
            pltpu.VMEM((hidden, depth), bf16),
            dma((3 + 2 * groups,)),
            dma((2, n - 1)),
            dma((2, n - 1)),
            dma((2, n)),
            dma((2, n)),
            dma((n, n - 1)),
            dma((n, n - 1)),
            dma((n, n - 1)),
            dma((n, n - 1)),
            dma((n,)),
            dma((n,)),
            dma((n - 1,)),
            dma((n - 1,)),
        ],
        compiler_params=pltpu.CompilerParams(
            collective_id=0, has_side_effects=True, vmem_limit_bytes=63 * 1024 * 1024
        ),
    )(tokens, out_grad, expert_ids.T, combine.T, w_gate[0], w_up[0], w_down[0])
    token_grad, gate_g, up_g, down_g = pl.pallas_call(
        functools.partial(hand_over, 4),
        out_shape=tuple(jax.ShapeDtypeStruct(result.shape, result.dtype) for result in results),
        in_specs=[hbm] * 4,
        out_specs=(hbm,) * 4,
        scratch_shapes=[pltpu.VMEM(result.shape, bf16) for result in results] + [dma((4,)), dma((4,))],
        compiler_params=pltpu.CompilerParams(vmem_limit_bytes=63 * 1024 * 1024),
    )(*results)
    return (token_grad, gate_g[None], up_g[None], down_g[None])


def fits_kernel(mesh):
    shape = mesh.shape
    return shape["section"] == 2 and shape["expert"] == 4 and shape["tp"] == 4


def solution(mesh):
    return jax.shard_map(
        on_device_kernel if fits_kernel(mesh) else on_device,
        mesh=mesh,
        in_specs=(
            P("expert", ("tp", "section")),
            P("expert", ("tp", "section")),
            P("expert", None),
            P("expert", None),
            P("expert", "tp", "section"),
            P("expert", "tp", "section"),
            P("expert", "section", "tp"),
        ),
        out_specs=(
            P("expert", ("tp", "section")),
            P("expert", "tp", "section"),
            P("expert", "tp", "section"),
            P("expert", "section", "tp"),
        ),
        check_vma=False,
    )
```

```python
import functools

import jax
import jax.numpy as jnp
from jax import lax
from jax.experimental import pallas as pl
from jax.experimental.pallas import tpu as pltpu
from jax.sharding import PartitionSpec as P

MESH = pl.DeviceIdType.MESH


def block_slots(expert_ids, experts, capacity):
    flat_ids = expert_ids.reshape(-1)
    pick_count = flat_ids.shape[0]
    onehot = (flat_ids[:, None] == jnp.arange(experts, dtype=jnp.int32)[None, :]).astype(jnp.int32)
    earlier = jnp.cumsum(onehot, axis=0) - onehot
    slot_index = jnp.sum(earlier * onehot, axis=1)
    place_index = flat_ids * capacity + slot_index
    source = (
        jnp.zeros((experts * capacity,), jnp.int32)
        .at[place_index]
        .set(jnp.arange(pick_count, dtype=jnp.int32))
    )
    filled = (
        jnp.zeros((experts * capacity,), jnp.int32)
        .at[place_index]
        .set(jnp.ones((pick_count,), jnp.int32))
    )
    return (slot_index, source.reshape(experts, capacity), filled.reshape(experts, capacity))


def round_back(values):
    return lax.optimization_barrier(values.astype(jnp.bfloat16)).astype(jnp.float32)


def local_grads(gate_pre, up_pre, hidden_grad):
    sigmoid_g = jax.nn.sigmoid(gate_pre)
    activated = (gate_pre * sigmoid_g * up_pre).astype(jnp.bfloat16)
    gate_grad = (hidden_grad * up_pre * sigmoid_g * (1.0 + gate_pre * (1.0 - sigmoid_g))).astype(
        jnp.bfloat16
    )
    up_grad = (hidden_grad * gate_pre * sigmoid_g).astype(jnp.bfloat16)
    return (activated, gate_grad, up_grad)


def fill_buffers(source, filled, combine, top_count, features, grad_rows):
    tok_count = features.shape[0]
    token_index = source // top_count
    keep_mask = (filled > 0)[:, :, None]
    positions = jnp.arange(tok_count, dtype=jnp.int32)[None, None, :]
    selector = jnp.logical_and(token_index[:, :, None] == positions, keep_mask).astype(jnp.bfloat16)
    rows_in = jnp.einsum(
        "ect,td->ecd", selector, features, preferred_element_type=jnp.float32
    ).astype(jnp.bfloat16)
    picked_grad = jnp.einsum("ect,td->ecd", selector, grad_rows, preferred_element_type=jnp.float32)
    weight = combine.reshape(-1)[source]
    grad_in = (picked_grad * weight[:, :, None]).astype(jnp.bfloat16)
    return (rows_in, grad_in)


def token_picker(pick_rows, tok_dev, top_count, row_count):
    columns = jnp.arange(row_count, dtype=jnp.int32)[None, None, :]
    hits = (pick_rows.reshape(tok_dev, top_count)[:, :, None] == columns).astype(jnp.int32)
    return jnp.sum(hits, axis=1)


def contract_rows(left_side, right_side):
    return lax.dot_general(
        left_side, right_side, (((0,), (0,)), ((), ())), preferred_element_type=jnp.float32
    )


def contract_last(left_side, right_side):
    return lax.dot_general(
        left_side, right_side, (((1,), (1,)), ((), ())), preferred_element_type=jnp.float32
    )


def on_device(tokens, out_grad, expert_ids, combine, w_gate, w_up, w_down):
    tok_dev, top_count = expert_ids.shape
    experts = lax.axis_size("expert")
    capacity = (tok_dev * top_count * 9 + 8 * experts - 1) // (8 * experts)
    slot_index, source, filled = block_slots(expert_ids, experts, capacity)
    features, grad_rows = (
        lax.all_gather(tokens, "section", axis=1, tiled=True),
        lax.all_gather(out_grad, "section", axis=1, tiled=True),
    )
    send_rows, send_grads = fill_buffers(source, filled, combine, top_count, features, grad_rows)
    got_rows, got_grads = (
        lax.all_to_all(send_rows, "expert", split_axis=0, concat_axis=0, tiled=True),
        lax.all_to_all(send_grads, "expert", split_axis=0, concat_axis=0, tiled=True),
    )
    width_dev = got_rows.shape[2]
    rows_in = got_rows.reshape(-1, width_dev)
    grad_in = got_grads.reshape(-1, width_dev)
    gate_w = w_gate[0]
    up_w = w_up[0]
    down_w = w_down[0]
    gate_part = round_back(jnp.dot(rows_in, gate_w, preferred_element_type=jnp.float32))
    up_part = round_back(jnp.dot(rows_in, up_w, preferred_element_type=jnp.float32))
    hidden_part = round_back(contract_last(grad_in, down_w))
    gate_pre, up_pre, hidden_grad = (
        lax.psum(gate_part.astype(jnp.bfloat16), "tp").astype(jnp.float32),
        lax.psum(up_part.astype(jnp.bfloat16), "tp").astype(jnp.float32),
        lax.psum(hidden_part.astype(jnp.bfloat16), "tp").astype(jnp.float32),
    )
    activated, gate_grad, up_grad = local_grads(gate_pre, up_pre, hidden_grad)
    row_float = contract_last(gate_grad, gate_w) + contract_last(up_grad, up_w)
    flat_ids = expert_ids.reshape(-1)
    pick_rows = flat_ids * capacity + slot_index
    picker = token_picker(pick_rows, tok_dev, top_count, experts * capacity)
    row_grad = row_float.astype(jnp.bfloat16)
    returned = lax.all_to_all(
        row_grad.reshape(experts, capacity, width_dev),
        "expert",
        split_axis=0,
        concat_axis=0,
        tiled=True,
    )
    summed = jnp.dot(
        picker.astype(jnp.bfloat16),
        returned.reshape(experts * capacity, width_dev),
        preferred_element_type=jnp.float32,
    )
    token_grad = lax.psum_scatter(
        summed.astype(jnp.bfloat16), "section", scatter_dimension=1, tiled=True
    )
    down_wgrad = contract_rows(activated, grad_in).astype(jnp.bfloat16)[None]
    gate_wgrad = contract_rows(rows_in, gate_grad).astype(jnp.bfloat16)[None]
    up_wgrad = contract_rows(rows_in, up_grad).astype(jnp.bfloat16)[None]
    return (token_grad, gate_wgrad, up_wgrad, down_wgrad)


def expert_kernel(
    n,
    slots,
    tok_hbm,
    grad_hbm,
    ids_ref,
    combine_ref,
    gate_hbm,
    up_hbm,
    down_hbm,
    token_out,
    gate_out,
    up_out,
    down_out,
    tok_ref,
    grad_ref,
    both_w,
    down_w,
    both_t,
    down_t,
    place_ref,
    weight_ref,
    picks,
    send_rows,
    send_grads,
    rows,
    grads,
    parts,
    got_parts,
    local,
    halves,
    got_half,
    back,
    returned,
    gate_g,
    up_g,
    down_g,
    io_sem,
    z_send,
    z_recv,
    s_send,
    s_recv,
    p_send,
    p_recv,
    a_send,
    a_recv,
    h_send,
    h_recv,
    r_send,
    r_recv,
):
    sec = lax.axis_index("section")
    exp = lax.axis_index("expert")
    tp = lax.axis_index("tp")
    other = 1 - sec
    tok_dev, width = tok_ref.shape
    hidden = down_w.shape[0]
    groups = hidden // 128
    share = parts.shape[1] // n
    sign = 2 * lax.rem(exp, 2) - 1

    def hop(axis, index):
        place = {"section": sec, "expert": exp, "tp": tp}
        place[axis] = index
        return (place["section"], place["expert"], place["tp"])

    def remote(src, dst, send, recv, target):
        return pltpu.make_async_remote_copy(
            src_ref=src,
            dst_ref=dst,
            send_sem=send,
            recv_sem=recv,
            device_id=target,
            device_id_type=MESH,
        )

    def partner(k):
        return lax.rem(exp + n + sign * k, n)

    fetch = [
        pltpu.make_async_copy(tok_hbm, tok_ref, io_sem.at[0]),
        pltpu.make_async_copy(grad_hbm, grad_ref, io_sem.at[1]),
    ]
    loads = [pltpu.make_async_copy(down_hbm, down_w, io_sem.at[2])]
    for j in range(groups):
        for index, source in enumerate((gate_hbm, up_hbm)):
            loads.append(
                pltpu.make_async_copy(
                    source.at[:, pl.ds(j * 128, 128)],
                    both_w.at[:, pl.ds((2 * j + index) * 128, 128)],
                    io_sem.at[3 + 2 * j + index],
                )
            )
    for copy in fetch + loads:
        copy.start()

    barrier = pltpu.get_barrier_semaphore()
    pl.semaphore_signal(barrier, inc=1, device_id=hop("section", other), device_id_type=MESH)
    for k in range(1, n):
        pl.semaphore_signal(barrier, inc=1, device_id=hop("expert", partner(k)), device_id_type=MESH)
        pl.semaphore_signal(
            barrier, inc=1, device_id=hop("tp", lax.rem(tp + k, n)), device_id_type=MESH
        )

    target = lax.rem(exp + 2 * n + sign * lax.rem(lax.broadcasted_iota(jnp.int32, (8, tok_dev), 0), n), n)
    first = ids_ref[0:1, :] == target
    second = ids_ref[1:2, :] == target
    named = jnp.logical_or(first, second).astype(jnp.float32)
    weight = jnp.where(first, combine_ref[0:1, :], 0.0) + jnp.where(second, combine_ref[1:2, :], 0.0)
    earlier = (
        lax.broadcasted_iota(jnp.int32, (tok_dev, tok_dev), 0)
        < lax.broadcasted_iota(jnp.int32, (tok_dev, tok_dev), 1)
    ).astype(jnp.bfloat16)
    slot = jnp.dot(named.astype(jnp.bfloat16), earlier, preferred_element_type=jnp.float32)
    place = jnp.where(named > 0.0, slot, -1.0)
    numbers = lax.broadcasted_iota(jnp.int32, (slots, tok_dev), 0).astype(jnp.float32)
    spare = n * share - groups * slots
    if spare > 0:
        for k in range(n):
            parts[k, groups * slots :, :] = jnp.zeros((spare, 384), jnp.bfloat16)

    def block(k):
        return pl.ds(pl.multiple_of(k * slots, 16), slots)

    def z_copies(k):
        goal = hop("expert", partner(k))
        return (
            remote(send_rows.at[k - 1], rows.at[sec, block(k)], z_send.at[0, k - 1], z_recv.at[0, k - 1], goal),
            remote(send_grads.at[k - 1], grads.at[sec, block(k)], z_send.at[1, k - 1], z_recv.at[1, k - 1], goal),
        )

    def s_copies(k):
        goal = hop("section", other)
        return (
            remote(rows.at[sec, block(k)], rows.at[sec, block(k)], s_send.at[0, k], s_recv.at[0, k], goal),
            remote(grads.at[sec, block(k)], grads.at[sec, block(k)], s_send.at[1, k], s_recv.at[1, k], goal),
        )

    def p_copy(k, r):
        goal = lax.rem(tp + r, n)
        span = pl.ds(pl.multiple_of(goal * share, share), share)
        return remote(
            parts.at[k, span], got_parts.at[k, r - 1], p_send.at[k, r - 1], p_recv.at[k, r - 1], hop("tp", goal)
        )

    mine = pl.ds(pl.multiple_of(tp * share, share), share)

    def a_copy(k, r):
        return remote(
            local.at[k, mine], local.at[k, mine], a_send.at[k, r - 1], a_recv.at[k, r - 1], hop("tp", lax.rem(tp + r, n))
        )

    def h_copy(k):
        return remote(halves.at[k], got_half.at[k], h_send.at[k], h_recv.at[k], hop("section", other))

    def r_copy(k):
        return remote(back.at[k - 1], returned.at[k], r_send.at[k - 1], r_recv.at[k - 1], hop("expert", partner(k)))

    far_first = (2, 1, 3)

    for copy in fetch:
        copy.wait()
    place_ref[...] = place
    weight_ref[...] = weight
    pl.semaphore_wait(barrier, 2 * n - 1)

    @pl.loop(0, n)
    def _(turn):
        k = jnp.where(turn == 0, 1, jnp.where(turn == 1, 3, jnp.where(turn == 2, 0, 2)))
        pick = (place_ref[pl.ds(k, 1), :] == numbers).astype(jnp.float32)
        spread = jnp.sum(pick * weight_ref[pl.ds(k, 1), :], axis=1, keepdims=True)
        pick = pick.astype(jnp.bfloat16)
        picks[k] = pick
        picked = jnp.dot(pick, tok_ref[...], preferred_element_type=jnp.float32).astype(jnp.bfloat16)

        @pl.when(k != 0)
        def _():
            send_rows[k - 1] = picked

        @pl.when(jnp.logical_and(k != 0, k != 2))
        def _():
            z_copies(k)[0].start()

        picked_grad = jnp.dot(pick, grad_ref[...], preferred_element_type=jnp.float32)
        picked_grad = (picked_grad * spread).astype(jnp.bfloat16)

        @pl.when(k == 0)
        def _():
            rows[sec, block(0)] = picked
            grads[sec, block(0)] = picked_grad
            for copy in s_copies(0):
                copy.start()

        @pl.when(k != 0)
        def _():
            send_grads[k - 1] = picked_grad

        @pl.when(jnp.logical_and(k != 0, k != 2))
        def _():
            z_copies(k)[1].start()

    for load in loads:
        load.wait()

    @pl.loop(0, 2 * width // 256)
    def _(index):
        span = pl.ds(pl.multiple_of(index * 256, 256), 256)
        both_t[:, span] = both_w[span, :].T
        down_t[span, :] = down_w[:, span].T


    def arrive(k):
        for copy, onward in zip(z_copies(k), s_copies(k)):
            copy.wait_recv()
            onward.start()

    def forward(k):
        for copy in s_copies(k):
            copy.wait_recv()
        pre = jnp.dot(rows[0, block(k)], both_w[0:width, :], preferred_element_type=jnp.float32)
        pre += jnp.dot(rows[1, block(k)], both_w[width : 2 * width, :], preferred_element_type=jnp.float32)
        inner = jnp.dot(grads[0, block(k)], down_t[0:width, :], preferred_element_type=jnp.float32)
        inner += jnp.dot(grads[1, block(k)], down_t[width : 2 * width, :], preferred_element_type=jnp.float32)
        for j in range(groups):
            parts[k, j * slots : (j + 1) * slots, 0:256] = pre[:, j * 256 : (j + 1) * 256].astype(jnp.bfloat16)
            parts[k, j * slots : (j + 1) * slots, 256:384] = inner[:, j * 128 : (j + 1) * 128].astype(jnp.bfloat16)
        for r in far_first:
            p_copy(k, r).start()

    def reduce_local(k):
        summed = parts[k, mine, :].astype(jnp.float32)
        for r in range(1, n):
            p_copy(k, r).wait_recv()
            summed += got_parts[k, r - 1].astype(jnp.float32)
        activated, gate_grad, up_grad = local_grads(summed[:, 0:128], summed[:, 128:256], summed[:, 256:384])
        local[k, mine, 0:128] = gate_grad
        local[k, mine, 128:256] = up_grad
        local[k, mine, 256:384] = activated
        for r in far_first:
            a_copy(k, r).start()

    def row_side(k, side):
        span = pl.ds(pl.multiple_of(side * width, width), width)
        return jnp.dot(gate_up(k), both_t[:, span], preferred_element_type=jnp.float32)

    def gate_up(k):
        return jnp.concatenate(
            [local[k, j * slots : (j + 1) * slots, 0:256] for j in range(groups)], axis=1
        )

    def active(k):
        return jnp.concatenate(
            [local[k, j * slots : (j + 1) * slots, 256:384] for j in range(groups)], axis=1
        )

    def backward(k):
        for r in range(1, n):
            a_copy(k, r).wait_recv()
        halves[k] = row_side(k, other).astype(jnp.bfloat16)
        h_copy(k).start()

    def give_back(k):
        own = row_side(k, sec)
        h_copy(k).wait_recv()
        whole = (own + got_half[k].astype(jnp.float32)).astype(jnp.bfloat16)

        @pl.when(k == 0)
        def _():
            returned[0] = whole

        @pl.when(k != 0)
        def _():
            back[k - 1] = whole
            r_copy(k).start()


    def nth(turn):
        return jnp.where(turn < 2, turn, n + 1 - turn)

    @pl.loop(0, n + 2)
    def _(turn):
        @pl.when(turn == 1)
        def _():
            for sent, copy in zip(z_copies(1), z_copies(2)):
                sent.wait_send()
                copy.start()

        @pl.when(jnp.logical_and(turn > 0, turn < n))
        def _():
            arrive(nth(turn))

        @pl.when(turn < n)
        def _():
            forward(nth(turn))

        @pl.when(jnp.logical_and(turn > 0, turn <= n))
        def _():
            reduce_local(nth(turn - 1))

        @pl.when(turn > 1)
        def _():
            give_back(nth(turn - 2))

        @pl.when(jnp.logical_and(turn > 0, turn <= n))
        def _():
            backward(nth(turn - 1))

    chunk = 256

    @pl.loop(0, 2 * width // chunk)
    def _(piece):
        per_side = width // chunk
        side = piece // per_side
        low = pl.ds(pl.multiple_of(lax.rem(piece, per_side) * chunk, chunk), chunk)
        span = pl.ds(pl.multiple_of(piece * chunk, chunk), chunk)
        total = sum(
            contract_rows(rows[side, block(k), low], gate_up(k)) for k in range(n)
        ).astype(jnp.bfloat16)
        for j in range(groups):
            gate_g[span, j * 128 : (j + 1) * 128] = total[:, j * 256 : j * 256 + 128]
            up_g[span, j * 128 : (j + 1) * 128] = total[:, j * 256 + 128 : (j + 1) * 256]
        down_g[:, span] = sum(
            contract_rows(active(k), grads[side, block(k), low]) for k in range(n)
        ).astype(jnp.bfloat16)

    stores = [
        pltpu.make_async_copy(gate_g, gate_out, io_sem.at[0]),
        pltpu.make_async_copy(up_g, up_out, io_sem.at[1]),
        pltpu.make_async_copy(down_g, down_out, io_sem.at[2]),
    ]
    for store in stores:
        store.start()

    total = contract_rows(picks[0], returned[0])
    for k in (1, 3, 2):
        r_copy(k).wait_recv()
        total += contract_rows(picks[k], returned[k])
    token_out[...] = total.astype(jnp.bfloat16)

    for k in range(n):
        for copy in s_copies(k):
            copy.wait_send()
        h_copy(k).wait_send()
        for r in range(1, n):
            p_copy(k, r).wait_send()
            a_copy(k, r).wait_send()
        if k > 0:
            if k > 1:
                for copy in z_copies(k):
                    copy.wait_send()
            r_copy(k).wait_send()
    for store in stores:
        store.wait()


def hand_over(count, *refs):
    sources, results, held = refs[:count], refs[count : 2 * count], refs[2 * count : 3 * count]
    load_sem, store_sem = refs[3 * count :]
    loads = [pltpu.make_async_copy(sources[i], held[i], load_sem.at[i]) for i in range(count)]
    stores = [pltpu.make_async_copy(held[i], results[i], store_sem.at[i]) for i in range(count)]
    for load in loads:
        load.start()
    for load, store in zip(loads, stores):
        load.wait()
        store.start()
    for store in stores:
        store.wait()


def on_device_kernel(tokens, out_grad, expert_ids, combine, w_gate, w_up, w_down):
    tok_dev, top_count = expert_ids.shape
    n = lax.axis_size("expert")
    capacity = (tok_dev * top_count * 9 + 8 * n - 1) // (8 * n)
    slots = (capacity + 15) // 16 * 16
    width = tokens.shape[1]
    depth, hidden = w_gate.shape[1:]
    groups = hidden // 128
    share = (groups * slots + 16 * n - 1) // (16 * n) * 16
    bf16 = jnp.bfloat16
    vmem = pl.BlockSpec(memory_space=pltpu.VMEM)
    hbm = pl.BlockSpec(memory_space=pl.ANY)
    dma = pltpu.SemaphoreType.DMA
    results = pl.pallas_call(
        functools.partial(expert_kernel, n, slots),
        out_shape=(
            jax.ShapeDtypeStruct((tok_dev, width), bf16),
            jax.ShapeDtypeStruct((depth, hidden), bf16),
            jax.ShapeDtypeStruct((depth, hidden), bf16),
            jax.ShapeDtypeStruct((hidden, depth), bf16),
        ),
        in_specs=[hbm, hbm, vmem, vmem, hbm, hbm, hbm],
        out_specs=(vmem, hbm, hbm, hbm),
        scratch_shapes=[
            pltpu.VMEM((tok_dev, width), bf16),
            pltpu.VMEM((tok_dev, width), bf16),
            pltpu.VMEM((depth, 2 * hidden), bf16),
            pltpu.VMEM((hidden, depth), bf16),
            pltpu.VMEM((2 * hidden, depth), bf16),
            pltpu.VMEM((depth, hidden), bf16),
            pltpu.VMEM((8, tok_dev), jnp.float32),
            pltpu.VMEM((8, tok_dev), jnp.float32),
            pltpu.VMEM((n, slots, tok_dev), bf16),
            pltpu.VMEM((n - 1, slots, width), bf16),
            pltpu.VMEM((n - 1, slots, width), bf16),
            pltpu.VMEM((2, n * slots, width), bf16),
            pltpu.VMEM((2, n * slots, width), bf16),
            pltpu.VMEM((n, n * share, 384), bf16),
            pltpu.VMEM((n, n - 1, share, 384), bf16),
            pltpu.VMEM((n, n * share, 384), bf16),
            pltpu.VMEM((n, slots, width), bf16),
            pltpu.VMEM((n, slots, width), bf16),
            pltpu.VMEM((n - 1, slots, width), bf16),
            pltpu.VMEM((n, slots, width), bf16),
            pltpu.VMEM((depth, hidden), bf16),
            pltpu.VMEM((depth, hidden), bf16),
            pltpu.VMEM((hidden, depth), bf16),
            dma((3 + 2 * groups,)),
            dma((2, n - 1)),
            dma((2, n - 1)),
            dma((2, n)),
            dma((2, n)),
            dma((n, n - 1)),
            dma((n, n - 1)),
            dma((n, n - 1)),
            dma((n, n - 1)),
            dma((n,)),
            dma((n,)),
            dma((n - 1,)),
            dma((n - 1,)),
        ],
        compiler_params=pltpu.CompilerParams(
            collective_id=0, has_side_effects=True, vmem_limit_bytes=63 * 1024 * 1024
        ),
    )(tokens, out_grad, expert_ids.T, combine.T, w_gate[0], w_up[0], w_down[0])
    token_grad, gate_g, up_g, down_g = pl.pallas_call(
        functools.partial(hand_over, 4),
        out_shape=tuple(jax.ShapeDtypeStruct(result.shape, result.dtype) for result in results),
        in_specs=[hbm] * 4,
        out_specs=(hbm,) * 4,
        scratch_shapes=[pltpu.VMEM(result.shape, bf16) for result in results] + [dma((4,)), dma((4,))],
        compiler_params=pltpu.CompilerParams(vmem_limit_bytes=63 * 1024 * 1024),
    )(*results)
    return (token_grad, gate_g[None], up_g[None], down_g[None])


def fits_kernel(mesh):
    shape = mesh.shape
    return shape["section"] == 2 and shape["expert"] == 4 and shape["tp"] == 4


def solution(mesh):
    return jax.shard_map(
        on_device_kernel if fits_kernel(mesh) else on_device,
        mesh=mesh,
        in_specs=(
            P("expert", ("tp", "section")),
            P("expert", ("tp", "section")),
            P("expert", None),
            P("expert", None),
            P("expert", "tp", "section"),
            P("expert", "tp", "section"),
            P("expert", "section", "tp"),
        ),
        out_specs=(
            P("expert", ("tp", "section")),
            P("expert", "tp", "section"),
            P("expert", "tp", "section"),
            P("expert", "section", "tp"),
        ),
        check_vma=False,
    )
```

```python
import functools

import jax
import jax.numpy as jnp
from jax import lax
from jax.experimental import pallas as pl
from jax.experimental.pallas import tpu as pltpu
from jax.sharding import PartitionSpec as P

MESH = pl.DeviceIdType.MESH


def block_slots(expert_ids, experts, capacity):
    flat_ids = expert_ids.reshape(-1)
    pick_count = flat_ids.shape[0]
    onehot = (flat_ids[:, None] == jnp.arange(experts, dtype=jnp.int32)[None, :]).astype(jnp.int32)
    earlier = jnp.cumsum(onehot, axis=0) - onehot
    slot_index = jnp.sum(earlier * onehot, axis=1)
    place_index = flat_ids * capacity + slot_index
    source = (
        jnp.zeros((experts * capacity,), jnp.int32)
        .at[place_index]
        .set(jnp.arange(pick_count, dtype=jnp.int32))
    )
    filled = (
        jnp.zeros((experts * capacity,), jnp.int32)
        .at[place_index]
        .set(jnp.ones((pick_count,), jnp.int32))
    )
    return (slot_index, source.reshape(experts, capacity), filled.reshape(experts, capacity))


def round_back(values):
    return lax.optimization_barrier(values.astype(jnp.bfloat16)).astype(jnp.float32)


def local_grads(gate_pre, up_pre, hidden_grad):
    sigmoid_g = jax.nn.sigmoid(gate_pre)
    activated = (gate_pre * sigmoid_g * up_pre).astype(jnp.bfloat16)
    gate_grad = (hidden_grad * up_pre * sigmoid_g * (1.0 + gate_pre * (1.0 - sigmoid_g))).astype(
        jnp.bfloat16
    )
    up_grad = (hidden_grad * gate_pre * sigmoid_g).astype(jnp.bfloat16)
    return (activated, gate_grad, up_grad)


def fill_buffers(source, filled, combine, top_count, features, grad_rows):
    tok_count = features.shape[0]
    token_index = source // top_count
    keep_mask = (filled > 0)[:, :, None]
    positions = jnp.arange(tok_count, dtype=jnp.int32)[None, None, :]
    selector = jnp.logical_and(token_index[:, :, None] == positions, keep_mask).astype(jnp.bfloat16)
    rows_in = jnp.einsum(
        "ect,td->ecd", selector, features, preferred_element_type=jnp.float32
    ).astype(jnp.bfloat16)
    picked_grad = jnp.einsum("ect,td->ecd", selector, grad_rows, preferred_element_type=jnp.float32)
    weight = combine.reshape(-1)[source]
    grad_in = (picked_grad * weight[:, :, None]).astype(jnp.bfloat16)
    return (rows_in, grad_in)


def token_picker(pick_rows, tok_dev, top_count, row_count):
    columns = jnp.arange(row_count, dtype=jnp.int32)[None, None, :]
    hits = (pick_rows.reshape(tok_dev, top_count)[:, :, None] == columns).astype(jnp.int32)
    return jnp.sum(hits, axis=1)


def contract_rows(left_side, right_side):
    return lax.dot_general(
        left_side, right_side, (((0,), (0,)), ((), ())), preferred_element_type=jnp.float32
    )


def contract_last(left_side, right_side):
    return lax.dot_general(
        left_side, right_side, (((1,), (1,)), ((), ())), preferred_element_type=jnp.float32
    )


def on_device(tokens, out_grad, expert_ids, combine, w_gate, w_up, w_down):
    tok_dev, top_count = expert_ids.shape
    experts = lax.axis_size("expert")
    capacity = (tok_dev * top_count * 9 + 8 * experts - 1) // (8 * experts)
    slot_index, source, filled = block_slots(expert_ids, experts, capacity)
    features, grad_rows = (
        lax.all_gather(tokens, "section", axis=1, tiled=True),
        lax.all_gather(out_grad, "section", axis=1, tiled=True),
    )
    send_rows, send_grads = fill_buffers(source, filled, combine, top_count, features, grad_rows)
    got_rows, got_grads = (
        lax.all_to_all(send_rows, "expert", split_axis=0, concat_axis=0, tiled=True),
        lax.all_to_all(send_grads, "expert", split_axis=0, concat_axis=0, tiled=True),
    )
    width_dev = got_rows.shape[2]
    rows_in = got_rows.reshape(-1, width_dev)
    grad_in = got_grads.reshape(-1, width_dev)
    gate_w = w_gate[0]
    up_w = w_up[0]
    down_w = w_down[0]
    gate_part = round_back(jnp.dot(rows_in, gate_w, preferred_element_type=jnp.float32))
    up_part = round_back(jnp.dot(rows_in, up_w, preferred_element_type=jnp.float32))
    hidden_part = round_back(contract_last(grad_in, down_w))
    gate_pre, up_pre, hidden_grad = (
        lax.psum(gate_part.astype(jnp.bfloat16), "tp").astype(jnp.float32),
        lax.psum(up_part.astype(jnp.bfloat16), "tp").astype(jnp.float32),
        lax.psum(hidden_part.astype(jnp.bfloat16), "tp").astype(jnp.float32),
    )
    activated, gate_grad, up_grad = local_grads(gate_pre, up_pre, hidden_grad)
    row_float = contract_last(gate_grad, gate_w) + contract_last(up_grad, up_w)
    flat_ids = expert_ids.reshape(-1)
    pick_rows = flat_ids * capacity + slot_index
    picker = token_picker(pick_rows, tok_dev, top_count, experts * capacity)
    row_grad = row_float.astype(jnp.bfloat16)
    returned = lax.all_to_all(
        row_grad.reshape(experts, capacity, width_dev),
        "expert",
        split_axis=0,
        concat_axis=0,
        tiled=True,
    )
    summed = jnp.dot(
        picker.astype(jnp.bfloat16),
        returned.reshape(experts * capacity, width_dev),
        preferred_element_type=jnp.float32,
    )
    token_grad = lax.psum_scatter(
        summed.astype(jnp.bfloat16), "section", scatter_dimension=1, tiled=True
    )
    down_wgrad = contract_rows(activated, grad_in).astype(jnp.bfloat16)[None]
    gate_wgrad = contract_rows(rows_in, gate_grad).astype(jnp.bfloat16)[None]
    up_wgrad = contract_rows(rows_in, up_grad).astype(jnp.bfloat16)[None]
    return (token_grad, gate_wgrad, up_wgrad, down_wgrad)


def expert_kernel(
    n,
    slots,
    tok_hbm,
    grad_hbm,
    ids_ref,
    combine_ref,
    gate_hbm,
    up_hbm,
    down_hbm,
    token_out,
    gate_out,
    up_out,
    down_out,
    tok_ref,
    grad_ref,
    both_w,
    down_w,
    both_t,
    down_t,
    place_ref,
    weight_ref,
    picks,
    send_rows,
    send_grads,
    rows,
    grads,
    parts,
    got_parts,
    local,
    halves,
    got_half,
    back,
    returned,
    gate_g,
    up_g,
    down_g,
    io_sem,
    z_send,
    z_recv,
    s_send,
    s_recv,
    p_send,
    p_recv,
    a_send,
    a_recv,
    h_send,
    h_recv,
    r_send,
    r_recv,
):
    sec = lax.axis_index("section")
    exp = lax.axis_index("expert")
    tp = lax.axis_index("tp")
    other = 1 - sec
    tok_dev, width = tok_ref.shape
    hidden = down_w.shape[0]
    groups = hidden // 128
    share = parts.shape[1] // n
    sign = 2 * lax.rem(exp, 2) - 1

    def hop(axis, index):
        place = {"section": sec, "expert": exp, "tp": tp}
        place[axis] = index
        return (place["section"], place["expert"], place["tp"])

    def remote(src, dst, send, recv, target):
        return pltpu.make_async_remote_copy(
            src_ref=src,
            dst_ref=dst,
            send_sem=send,
            recv_sem=recv,
            device_id=target,
            device_id_type=MESH,
        )

    def partner(k):
        return lax.rem(exp + n + sign * k, n)

    fetch = [
        pltpu.make_async_copy(tok_hbm, tok_ref, io_sem.at[0]),
        pltpu.make_async_copy(grad_hbm, grad_ref, io_sem.at[1]),
    ]
    loads = [pltpu.make_async_copy(down_hbm, down_w, io_sem.at[2])]
    for j in range(groups):
        for index, source in enumerate((gate_hbm, up_hbm)):
            loads.append(
                pltpu.make_async_copy(
                    source.at[:, pl.ds(j * 128, 128)],
                    both_w.at[:, pl.ds((2 * j + index) * 128, 128)],
                    io_sem.at[3 + 2 * j + index],
                )
            )
    for copy in fetch + loads:
        copy.start()

    barrier = pltpu.get_barrier_semaphore()
    pl.semaphore_signal(barrier, inc=1, device_id=hop("section", other), device_id_type=MESH)
    for k in range(1, n):
        pl.semaphore_signal(barrier, inc=1, device_id=hop("expert", partner(k)), device_id_type=MESH)
        pl.semaphore_signal(
            barrier, inc=1, device_id=hop("tp", lax.rem(tp + k, n)), device_id_type=MESH
        )

    target = lax.rem(exp + 2 * n + sign * lax.rem(lax.broadcasted_iota(jnp.int32, (8, tok_dev), 0), n), n)
    first = ids_ref[0:1, :] == target
    second = ids_ref[1:2, :] == target
    named = jnp.logical_or(first, second).astype(jnp.float32)
    weight = jnp.where(first, combine_ref[0:1, :], 0.0) + jnp.where(second, combine_ref[1:2, :], 0.0)
    earlier = (
        lax.broadcasted_iota(jnp.int32, (tok_dev, tok_dev), 0)
        < lax.broadcasted_iota(jnp.int32, (tok_dev, tok_dev), 1)
    ).astype(jnp.bfloat16)
    slot = jnp.dot(named.astype(jnp.bfloat16), earlier, preferred_element_type=jnp.float32)
    place = jnp.where(named > 0.0, slot, -1.0)
    numbers = lax.broadcasted_iota(jnp.int32, (slots, tok_dev), 0).astype(jnp.float32)
    spare = n * share - groups * slots
    if spare > 0:
        for k in range(n):
            parts[k, groups * slots :, :] = jnp.zeros((spare, 384), jnp.bfloat16)

    def block(k):
        return pl.ds(pl.multiple_of(k * slots, 16), slots)

    def z_copies(k):
        goal = hop("expert", partner(k))
        return (
            remote(send_rows.at[k - 1], rows.at[sec, block(k)], z_send.at[0, k - 1], z_recv.at[0, k - 1], goal),
            remote(send_grads.at[k - 1], grads.at[sec, block(k)], z_send.at[1, k - 1], z_recv.at[1, k - 1], goal),
        )

    def s_copies(k):
        goal = hop("section", other)
        return (
            remote(rows.at[sec, block(k)], rows.at[sec, block(k)], s_send.at[0, k], s_recv.at[0, k], goal),
            remote(grads.at[sec, block(k)], grads.at[sec, block(k)], s_send.at[1, k], s_recv.at[1, k], goal),
        )

    def p_copy(k, r):
        goal = lax.rem(tp + r, n)
        span = pl.ds(pl.multiple_of(goal * share, share), share)
        return remote(
            parts.at[k, span], got_parts.at[k, r - 1], p_send.at[k, r - 1], p_recv.at[k, r - 1], hop("tp", goal)
        )

    mine = pl.ds(pl.multiple_of(tp * share, share), share)

    def a_copy(k, r):
        return remote(
            local.at[k, mine], local.at[k, mine], a_send.at[k, r - 1], a_recv.at[k, r - 1], hop("tp", lax.rem(tp + r, n))
        )

    def h_copy(k):
        return remote(halves.at[k], got_half.at[k], h_send.at[k], h_recv.at[k], hop("section", other))

    def r_copy(k):
        return remote(back.at[k - 1], returned.at[k], r_send.at[k - 1], r_recv.at[k - 1], hop("expert", partner(k)))

    far_first = (2, 1, 3)

    for copy in fetch:
        copy.wait()
    place_ref[...] = place
    weight_ref[...] = weight
    pl.semaphore_wait(barrier, 2 * n - 1)

    @pl.loop(1, n + 1)
    def _(turn):
        k = lax.rem(turn, n)
        pick = (place_ref[pl.ds(k, 1), :] == numbers).astype(jnp.float32)
        spread = jnp.sum(pick * weight_ref[pl.ds(k, 1), :], axis=1, keepdims=True)
        pick = pick.astype(jnp.bfloat16)
        picks[k] = pick
        picked = jnp.dot(pick, tok_ref[...], preferred_element_type=jnp.float32).astype(jnp.bfloat16)
        picked_grad = jnp.dot(pick, grad_ref[...], preferred_element_type=jnp.float32)
        picked_grad = (picked_grad * spread).astype(jnp.bfloat16)

        @pl.when(k == 0)
        def _():
            rows[sec, block(0)] = picked
            grads[sec, block(0)] = picked_grad
            for copy in s_copies(0):
                copy.start()

        @pl.when(k != 0)
        def _():
            send_rows[k - 1] = picked
            send_grads[k - 1] = picked_grad
            for copy in z_copies(k):
                copy.start()

    for load in loads:
        load.wait()

    @pl.loop(0, 2 * width // 256)
    def _(index):
        span = pl.ds(pl.multiple_of(index * 256, 256), 256)
        down_t[span, :] = down_w[:, span].T


    def arrive(k):
        for copy, onward in zip(z_copies(k), s_copies(k)):
            copy.wait_recv()
            onward.start()

    def forward(k):
        for copy in s_copies(k):
            copy.wait_recv()
        pre = jnp.dot(rows[0, block(k)], both_w[0:width, :], preferred_element_type=jnp.float32)
        pre += jnp.dot(rows[1, block(k)], both_w[width : 2 * width, :], preferred_element_type=jnp.float32)
        inner = jnp.dot(grads[0, block(k)], down_t[0:width, :], preferred_element_type=jnp.float32)
        inner += jnp.dot(grads[1, block(k)], down_t[width : 2 * width, :], preferred_element_type=jnp.float32)
        for j in range(groups):
            parts[k, j * slots : (j + 1) * slots, 0:256] = pre[:, j * 256 : (j + 1) * 256].astype(jnp.bfloat16)
            parts[k, j * slots : (j + 1) * slots, 256:384] = inner[:, j * 128 : (j + 1) * 128].astype(jnp.bfloat16)
        for r in far_first:
            p_copy(k, r).start()

    def reduce_local(k):
        summed = parts[k, mine, :].astype(jnp.float32)
        for r in range(1, n):
            p_copy(k, r).wait_recv()
            summed += got_parts[k, r - 1].astype(jnp.float32)
        activated, gate_grad, up_grad = local_grads(summed[:, 0:128], summed[:, 128:256], summed[:, 256:384])
        local[k, mine, 0:128] = gate_grad
        local[k, mine, 128:256] = up_grad
        local[k, mine, 256:384] = activated
        for r in far_first:
            a_copy(k, r).start()

    def row_side(k, side):
        span = pl.ds(pl.multiple_of(side * width, width), width)
        return jnp.dot(gate_up(k), both_t[:, span], preferred_element_type=jnp.float32)

    def gate_up(k):
        return jnp.concatenate(
            [local[k, j * slots : (j + 1) * slots, 0:256] for j in range(groups)], axis=1
        )

    def active(k):
        return jnp.concatenate(
            [local[k, j * slots : (j + 1) * slots, 256:384] for j in range(groups)], axis=1
        )

    def backward(k):
        for r in range(1, n):
            a_copy(k, r).wait_recv()
        halves[k] = row_side(k, other).astype(jnp.bfloat16)
        h_copy(k).start()

    def give_back(k):
        own = row_side(k, sec)
        h_copy(k).wait_recv()
        whole = (own + got_half[k].astype(jnp.float32)).astype(jnp.bfloat16)

        @pl.when(k == 0)
        def _():
            returned[0] = whole

        @pl.when(k != 0)
        def _():
            back[k - 1] = whole
            r_copy(k).start()


    def nth(turn):
        return jnp.where(turn < 2, turn, n + 1 - turn)

    @pl.loop(0, n + 2)
    def _(turn):
        @pl.when(jnp.logical_and(turn > 0, turn < n))
        def _():
            arrive(nth(turn))

        @pl.when(jnp.logical_and(turn > 0, turn <= n))
        def _():
            reduce_local(nth(turn - 1))

        @pl.when(turn < n)
        def _():
            forward(nth(turn))

        @pl.when(turn == 0)
        def _():
            @pl.loop(0, 2 * width // 256)
            def _(index):
                span = pl.ds(pl.multiple_of(index * 256, 256), 256)
                both_t[:, span] = both_w[span, :].T

        @pl.when(turn > 1)
        def _():
            give_back(nth(turn - 2))

        @pl.when(jnp.logical_and(turn > 0, turn <= n))
        def _():
            backward(nth(turn - 1))

    chunk = 256

    @pl.loop(0, 2 * width // chunk)
    def _(piece):
        per_side = width // chunk
        side = piece // per_side
        low = pl.ds(pl.multiple_of(lax.rem(piece, per_side) * chunk, chunk), chunk)
        span = pl.ds(pl.multiple_of(piece * chunk, chunk), chunk)
        total = contract_rows(
            rows[side, :, low], jnp.concatenate([gate_up(k) for k in range(n)], axis=0)
        ).astype(jnp.bfloat16)
        for j in range(groups):
            gate_g[span, j * 128 : (j + 1) * 128] = total[:, j * 256 : j * 256 + 128]
            up_g[span, j * 128 : (j + 1) * 128] = total[:, j * 256 + 128 : (j + 1) * 256]
        down_g[:, span] = contract_rows(
            jnp.concatenate([active(k) for k in range(n)], axis=0), grads[side, :, low]
        ).astype(jnp.bfloat16)

    stores = [
        pltpu.make_async_copy(gate_g, gate_out, io_sem.at[0]),
        pltpu.make_async_copy(up_g, up_out, io_sem.at[1]),
        pltpu.make_async_copy(down_g, down_out, io_sem.at[2]),
    ]
    for store in stores:
        store.start()

    total = contract_rows(picks[0], returned[0])
    for k in (1, 3, 2):
        r_copy(k).wait_recv()
        total += contract_rows(picks[k], returned[k])
    token_out[...] = total.astype(jnp.bfloat16)

    for k in range(n):
        for copy in s_copies(k):
            copy.wait_send()
        h_copy(k).wait_send()
        for r in range(1, n):
            p_copy(k, r).wait_send()
            a_copy(k, r).wait_send()
        if k > 0:
            for copy in z_copies(k):
                copy.wait_send()
            r_copy(k).wait_send()
    for store in stores:
        store.wait()


def hand_over(count, *refs):
    sources, results, held = refs[:count], refs[count : 2 * count], refs[2 * count : 3 * count]
    load_sem, store_sem = refs[3 * count :]
    loads = [pltpu.make_async_copy(sources[i], held[i], load_sem.at[i]) for i in range(count)]
    stores = [pltpu.make_async_copy(held[i], results[i], store_sem.at[i]) for i in range(count)]
    for load in loads:
        load.start()
    for load, store in zip(loads, stores):
        load.wait()
        store.start()
    for store in stores:
        store.wait()


def on_device_kernel(tokens, out_grad, expert_ids, combine, w_gate, w_up, w_down):
    tok_dev, top_count = expert_ids.shape
    n = lax.axis_size("expert")
    capacity = (tok_dev * top_count * 9 + 8 * n - 1) // (8 * n)
    slots = (capacity + 15) // 16 * 16
    width = tokens.shape[1]
    depth, hidden = w_gate.shape[1:]
    groups = hidden // 128
    share = (groups * slots + 16 * n - 1) // (16 * n) * 16
    bf16 = jnp.bfloat16
    vmem = pl.BlockSpec(memory_space=pltpu.VMEM)
    hbm = pl.BlockSpec(memory_space=pl.ANY)
    dma = pltpu.SemaphoreType.DMA
    results = pl.pallas_call(
        functools.partial(expert_kernel, n, slots),
        out_shape=(
            jax.ShapeDtypeStruct((tok_dev, width), bf16),
            jax.ShapeDtypeStruct((depth, hidden), bf16),
            jax.ShapeDtypeStruct((depth, hidden), bf16),
            jax.ShapeDtypeStruct((hidden, depth), bf16),
        ),
        in_specs=[hbm, hbm, vmem, vmem, hbm, hbm, hbm],
        out_specs=(vmem, hbm, hbm, hbm),
        scratch_shapes=[
            pltpu.VMEM((tok_dev, width), bf16),
            pltpu.VMEM((tok_dev, width), bf16),
            pltpu.VMEM((depth, 2 * hidden), bf16),
            pltpu.VMEM((hidden, depth), bf16),
            pltpu.VMEM((2 * hidden, depth), bf16),
            pltpu.VMEM((depth, hidden), bf16),
            pltpu.VMEM((8, tok_dev), jnp.float32),
            pltpu.VMEM((8, tok_dev), jnp.float32),
            pltpu.VMEM((n, slots, tok_dev), bf16),
            pltpu.VMEM((n - 1, slots, width), bf16),
            pltpu.VMEM((n - 1, slots, width), bf16),
            pltpu.VMEM((2, n * slots, width), bf16),
            pltpu.VMEM((2, n * slots, width), bf16),
            pltpu.VMEM((n, n * share, 384), bf16),
            pltpu.VMEM((n, n - 1, share, 384), bf16),
            pltpu.VMEM((n, n * share, 384), bf16),
            pltpu.VMEM((n, slots, width), bf16),
            pltpu.VMEM((n, slots, width), bf16),
            pltpu.VMEM((n - 1, slots, width), bf16),
            pltpu.VMEM((n, slots, width), bf16),
            pltpu.VMEM((depth, hidden), bf16),
            pltpu.VMEM((depth, hidden), bf16),
            pltpu.VMEM((hidden, depth), bf16),
            dma((3 + 2 * groups,)),
            dma((2, n - 1)),
            dma((2, n - 1)),
            dma((2, n)),
            dma((2, n)),
            dma((n, n - 1)),
            dma((n, n - 1)),
            dma((n, n - 1)),
            dma((n, n - 1)),
            dma((n,)),
            dma((n,)),
            dma((n - 1,)),
            dma((n - 1,)),
        ],
        compiler_params=pltpu.CompilerParams(
            collective_id=0, has_side_effects=True, vmem_limit_bytes=63 * 1024 * 1024
        ),
    )(tokens, out_grad, expert_ids.T, combine.T, w_gate[0], w_up[0], w_down[0])
    token_grad, gate_g, up_g, down_g = pl.pallas_call(
        functools.partial(hand_over, 4),
        out_shape=tuple(jax.ShapeDtypeStruct(result.shape, result.dtype) for result in results),
        in_specs=[hbm] * 4,
        out_specs=(hbm,) * 4,
        scratch_shapes=[pltpu.VMEM(result.shape, bf16) for result in results] + [dma((4,)), dma((4,))],
        compiler_params=pltpu.CompilerParams(vmem_limit_bytes=63 * 1024 * 1024),
    )(*results)
    return (token_grad, gate_g[None], up_g[None], down_g[None])


def fits_kernel(mesh):
    shape = mesh.shape
    return shape["section"] == 2 and shape["expert"] == 4 and shape["tp"] == 4


def solution(mesh):
    return jax.shard_map(
        on_device_kernel if fits_kernel(mesh) else on_device,
        mesh=mesh,
        in_specs=(
            P("expert", ("tp", "section")),
            P("expert", ("tp", "section")),
            P("expert", None),
            P("expert", None),
            P("expert", "tp", "section"),
            P("expert", "tp", "section"),
            P("expert", "section", "tp"),
        ),
        out_specs=(
            P("expert", ("tp", "section")),
            P("expert", "tp", "section"),
            P("expert", "tp", "section"),
            P("expert", "section", "tp"),
        ),
        check_vma=False,
    )
```

```python
import functools

import jax
import jax.numpy as jnp
from jax import lax
from jax.experimental import pallas as pl
from jax.experimental.pallas import tpu as pltpu
from jax.sharding import PartitionSpec as P

MESH = pl.DeviceIdType.MESH


def block_slots(expert_ids, experts, capacity):
    flat_ids = expert_ids.reshape(-1)
    pick_count = flat_ids.shape[0]
    onehot = (flat_ids[:, None] == jnp.arange(experts, dtype=jnp.int32)[None, :]).astype(jnp.int32)
    earlier = jnp.cumsum(onehot, axis=0) - onehot
    slot_index = jnp.sum(earlier * onehot, axis=1)
    place_index = flat_ids * capacity + slot_index
    source = (
        jnp.zeros((experts * capacity,), jnp.int32)
        .at[place_index]
        .set(jnp.arange(pick_count, dtype=jnp.int32))
    )
    filled = (
        jnp.zeros((experts * capacity,), jnp.int32)
        .at[place_index]
        .set(jnp.ones((pick_count,), jnp.int32))
    )
    return (slot_index, source.reshape(experts, capacity), filled.reshape(experts, capacity))


def round_back(values):
    return lax.optimization_barrier(values.astype(jnp.bfloat16)).astype(jnp.float32)


def local_grads(gate_pre, up_pre, hidden_grad):
    sigmoid_g = jax.nn.sigmoid(gate_pre)
    activated = (gate_pre * sigmoid_g * up_pre).astype(jnp.bfloat16)
    gate_grad = (hidden_grad * up_pre * sigmoid_g * (1.0 + gate_pre * (1.0 - sigmoid_g))).astype(
        jnp.bfloat16
    )
    up_grad = (hidden_grad * gate_pre * sigmoid_g).astype(jnp.bfloat16)
    return (activated, gate_grad, up_grad)


def fill_buffers(source, filled, combine, top_count, features, grad_rows):
    tok_count = features.shape[0]
    token_index = source // top_count
    keep_mask = (filled > 0)[:, :, None]
    positions = jnp.arange(tok_count, dtype=jnp.int32)[None, None, :]
    selector = jnp.logical_and(token_index[:, :, None] == positions, keep_mask).astype(jnp.bfloat16)
    rows_in = jnp.einsum(
        "ect,td->ecd", selector, features, preferred_element_type=jnp.float32
    ).astype(jnp.bfloat16)
    picked_grad = jnp.einsum("ect,td->ecd", selector, grad_rows, preferred_element_type=jnp.float32)
    weight = combine.reshape(-1)[source]
    grad_in = (picked_grad * weight[:, :, None]).astype(jnp.bfloat16)
    return (rows_in, grad_in)


def token_picker(pick_rows, tok_dev, top_count, row_count):
    columns = jnp.arange(row_count, dtype=jnp.int32)[None, None, :]
    hits = (pick_rows.reshape(tok_dev, top_count)[:, :, None] == columns).astype(jnp.int32)
    return jnp.sum(hits, axis=1)


def contract_rows(left_side, right_side):
    return lax.dot_general(
        left_side, right_side, (((0,), (0,)), ((), ())), preferred_element_type=jnp.float32
    )


def contract_last(left_side, right_side):
    return lax.dot_general(
        left_side, right_side, (((1,), (1,)), ((), ())), preferred_element_type=jnp.float32
    )


def on_device(tokens, out_grad, expert_ids, combine, w_gate, w_up, w_down):
    tok_dev, top_count = expert_ids.shape
    experts = lax.axis_size("expert")
    capacity = (tok_dev * top_count * 9 + 8 * experts - 1) // (8 * experts)
    slot_index, source, filled = block_slots(expert_ids, experts, capacity)
    features, grad_rows = (
        lax.all_gather(tokens, "section", axis=1, tiled=True),
        lax.all_gather(out_grad, "section", axis=1, tiled=True),
    )
    send_rows, send_grads = fill_buffers(source, filled, combine, top_count, features, grad_rows)
    got_rows, got_grads = (
        lax.all_to_all(send_rows, "expert", split_axis=0, concat_axis=0, tiled=True),
        lax.all_to_all(send_grads, "expert", split_axis=0, concat_axis=0, tiled=True),
    )
    width_dev = got_rows.shape[2]
    rows_in = got_rows.reshape(-1, width_dev)
    grad_in = got_grads.reshape(-1, width_dev)
    gate_w = w_gate[0]
    up_w = w_up[0]
    down_w = w_down[0]
    gate_part = round_back(jnp.dot(rows_in, gate_w, preferred_element_type=jnp.float32))
    up_part = round_back(jnp.dot(rows_in, up_w, preferred_element_type=jnp.float32))
    hidden_part = round_back(contract_last(grad_in, down_w))
    gate_pre, up_pre, hidden_grad = (
        lax.psum(gate_part.astype(jnp.bfloat16), "tp").astype(jnp.float32),
        lax.psum(up_part.astype(jnp.bfloat16), "tp").astype(jnp.float32),
        lax.psum(hidden_part.astype(jnp.bfloat16), "tp").astype(jnp.float32),
    )
    activated, gate_grad, up_grad = local_grads(gate_pre, up_pre, hidden_grad)
    row_float = contract_last(gate_grad, gate_w) + contract_last(up_grad, up_w)
    flat_ids = expert_ids.reshape(-1)
    pick_rows = flat_ids * capacity + slot_index
    picker = token_picker(pick_rows, tok_dev, top_count, experts * capacity)
    row_grad = row_float.astype(jnp.bfloat16)
    returned = lax.all_to_all(
        row_grad.reshape(experts, capacity, width_dev),
        "expert",
        split_axis=0,
        concat_axis=0,
        tiled=True,
    )
    summed = jnp.dot(
        picker.astype(jnp.bfloat16),
        returned.reshape(experts * capacity, width_dev),
        preferred_element_type=jnp.float32,
    )
    token_grad = lax.psum_scatter(
        summed.astype(jnp.bfloat16), "section", scatter_dimension=1, tiled=True
    )
    down_wgrad = contract_rows(activated, grad_in).astype(jnp.bfloat16)[None]
    gate_wgrad = contract_rows(rows_in, gate_grad).astype(jnp.bfloat16)[None]
    up_wgrad = contract_rows(rows_in, up_grad).astype(jnp.bfloat16)[None]
    return (token_grad, gate_wgrad, up_wgrad, down_wgrad)


def expert_kernel(
    n,
    slots,
    tok_hbm,
    grad_hbm,
    ids_ref,
    combine_ref,
    gate_hbm,
    up_hbm,
    down_hbm,
    token_out,
    gate_out,
    up_out,
    down_out,
    tok_ref,
    grad_ref,
    both_w,
    down_w,
    both_t,
    down_t,
    place_ref,
    weight_ref,
    picks,
    send_rows,
    send_grads,
    rows,
    grads,
    parts,
    got_parts,
    local,
    halves,
    got_half,
    back,
    returned,
    gate_g,
    up_g,
    down_g,
    io_sem,
    z_send,
    z_recv,
    s_send,
    s_recv,
    p_send,
    p_recv,
    a_send,
    a_recv,
    h_send,
    h_recv,
    r_send,
    r_recv,
):
    sec = lax.axis_index("section")
    exp = lax.axis_index("expert")
    tp = lax.axis_index("tp")
    other = 1 - sec
    tok_dev, width = tok_ref.shape
    hidden = down_w.shape[0]
    groups = hidden // 128
    share = parts.shape[1] // n
    sign = 2 * lax.rem(exp, 2) - 1

    def hop(axis, index):
        place = {"section": sec, "expert": exp, "tp": tp}
        place[axis] = index
        return (place["section"], place["expert"], place["tp"])

    def remote(src, dst, send, recv, target):
        return pltpu.make_async_remote_copy(
            src_ref=src,
            dst_ref=dst,
            send_sem=send,
            recv_sem=recv,
            device_id=target,
            device_id_type=MESH,
        )

    def partner(k):
        return lax.rem(exp + n + sign * k, n)

    fetch = [
        pltpu.make_async_copy(tok_hbm, tok_ref, io_sem.at[0]),
        pltpu.make_async_copy(grad_hbm, grad_ref, io_sem.at[1]),
    ]
    loads = [pltpu.make_async_copy(down_hbm, down_w, io_sem.at[2])]
    for j in range(groups):
        for index, source in enumerate((gate_hbm, up_hbm)):
            loads.append(
                pltpu.make_async_copy(
                    source.at[:, pl.ds(j * 128, 128)],
                    both_w.at[:, pl.ds((2 * j + index) * 128, 128)],
                    io_sem.at[3 + 2 * j + index],
                )
            )
    for copy in fetch + loads:
        copy.start()

    barrier = pltpu.get_barrier_semaphore()
    pl.semaphore_signal(barrier, inc=1, device_id=hop("section", other), device_id_type=MESH)
    for k in range(1, n):
        pl.semaphore_signal(barrier, inc=1, device_id=hop("expert", partner(k)), device_id_type=MESH)
        pl.semaphore_signal(
            barrier, inc=1, device_id=hop("tp", lax.rem(tp + k, n)), device_id_type=MESH
        )

    target = lax.rem(exp + 2 * n + sign * lax.rem(lax.broadcasted_iota(jnp.int32, (8, tok_dev), 0), n), n)
    first = ids_ref[0:1, :] == target
    second = ids_ref[1:2, :] == target
    named = jnp.logical_or(first, second).astype(jnp.float32)
    weight = jnp.where(first, combine_ref[0:1, :], 0.0) + jnp.where(second, combine_ref[1:2, :], 0.0)
    earlier = (
        lax.broadcasted_iota(jnp.int32, (tok_dev, tok_dev), 0)
        < lax.broadcasted_iota(jnp.int32, (tok_dev, tok_dev), 1)
    ).astype(jnp.bfloat16)
    slot = jnp.dot(named.astype(jnp.bfloat16), earlier, preferred_element_type=jnp.float32)
    place = jnp.where(named > 0.0, slot, -1.0)
    numbers = lax.broadcasted_iota(jnp.int32, (slots, tok_dev), 0).astype(jnp.float32)
    spare = n * share - groups * slots
    if spare > 0:
        for k in range(n):
            parts[k, groups * slots :, :] = jnp.zeros((spare, 384), jnp.bfloat16)

    def block(k):
        return pl.ds(pl.multiple_of(k * slots, 16), slots)

    def z_copies(k):
        goal = hop("expert", partner(k))
        return (
            remote(send_rows.at[k - 1], rows.at[sec, block(k)], z_send.at[0, k - 1], z_recv.at[0, k - 1], goal),
            remote(send_grads.at[k - 1], grads.at[sec, block(k)], z_send.at[1, k - 1], z_recv.at[1, k - 1], goal),
        )

    def s_copies(k):
        goal = hop("section", other)
        return (
            remote(rows.at[sec, block(k)], rows.at[sec, block(k)], s_send.at[0, k], s_recv.at[0, k], goal),
            remote(grads.at[sec, block(k)], grads.at[sec, block(k)], s_send.at[1, k], s_recv.at[1, k], goal),
        )

    def p_copy(k, r):
        goal = lax.rem(tp + r, n)
        span = pl.ds(pl.multiple_of(goal * share, share), share)
        return remote(
            parts.at[k, span], got_parts.at[k, r - 1], p_send.at[k, r - 1], p_recv.at[k, r - 1], hop("tp", goal)
        )

    mine = pl.ds(pl.multiple_of(tp * share, share), share)

    def a_copy(k, r):
        return remote(
            local.at[k, mine], local.at[k, mine], a_send.at[k, r - 1], a_recv.at[k, r - 1], hop("tp", lax.rem(tp + r, n))
        )

    def h_copy(k):
        return remote(halves.at[k], got_half.at[k], h_send.at[k], h_recv.at[k], hop("section", other))

    def r_copy(k):
        return remote(back.at[k - 1], returned.at[k], r_send.at[k - 1], r_recv.at[k - 1], hop("expert", partner(k)))

    far_first = (2, 1, 3)

    for copy in fetch:
        copy.wait()
    place_ref[...] = place
    weight_ref[...] = weight
    pl.semaphore_wait(barrier, 2 * n - 1)

    @pl.loop(1, n + 1)
    def _(turn):
        k = lax.rem(turn, n)
        pick = (place_ref[pl.ds(k, 1), :] == numbers).astype(jnp.float32)
        spread = jnp.sum(pick * weight_ref[pl.ds(k, 1), :], axis=1, keepdims=True)
        pick = pick.astype(jnp.bfloat16)
        picks[k] = pick
        picked = jnp.dot(pick, tok_ref[...], preferred_element_type=jnp.float32).astype(jnp.bfloat16)
        picked_grad = jnp.dot(pick, grad_ref[...], preferred_element_type=jnp.float32)
        picked_grad = (picked_grad * spread).astype(jnp.bfloat16)

        @pl.when(k == 0)
        def _():
            rows[sec, block(0)] = picked
            grads[sec, block(0)] = picked_grad
            for copy in s_copies(0):
                copy.start()

        @pl.when(k != 0)
        def _():
            send_rows[k - 1] = picked
            send_grads[k - 1] = picked_grad
            for copy in z_copies(k):
                copy.start()

    for load in loads:
        load.wait()

    @pl.loop(0, 2 * width // 256)
    def _(index):
        span = pl.ds(pl.multiple_of(index * 256, 256), 256)
        down_t[span, :] = down_w[:, span].T


    def arrive(k):
        for copy, onward in zip(z_copies(k), s_copies(k)):
            copy.wait_recv()
            onward.start()

    def forward(k):
        for copy in s_copies(k):
            copy.wait_recv()
        pre = jnp.dot(rows[0, block(k)], both_w[0:width, :], preferred_element_type=jnp.float32)
        pre += jnp.dot(rows[1, block(k)], both_w[width : 2 * width, :], preferred_element_type=jnp.float32)
        inner = jnp.dot(grads[0, block(k)], down_t[0:width, :], preferred_element_type=jnp.float32)
        inner += jnp.dot(grads[1, block(k)], down_t[width : 2 * width, :], preferred_element_type=jnp.float32)
        for j in range(groups):
            parts[k, j * slots : (j + 1) * slots, 0:256] = pre[:, j * 256 : (j + 1) * 256].astype(jnp.bfloat16)
            parts[k, j * slots : (j + 1) * slots, 256:384] = inner[:, j * 128 : (j + 1) * 128].astype(jnp.bfloat16)
        for r in far_first:
            p_copy(k, r).start()

    def reduce_local(k):
        summed = parts[k, mine, :].astype(jnp.float32)
        for r in range(1, n):
            p_copy(k, r).wait_recv()
            summed += got_parts[k, r - 1].astype(jnp.float32)
        activated, gate_grad, up_grad = local_grads(summed[:, 0:128], summed[:, 128:256], summed[:, 256:384])
        local[k, mine, 0:128] = gate_grad
        local[k, mine, 128:256] = up_grad
        local[k, mine, 256:384] = activated
        for r in far_first:
            a_copy(k, r).start()

    def row_side(k, side):
        span = pl.ds(pl.multiple_of(side * width, width), width)
        return jnp.dot(gate_up(k), both_t[:, span], preferred_element_type=jnp.float32)

    def gate_up(k):
        return jnp.concatenate(
            [local[k, j * slots : (j + 1) * slots, 0:256] for j in range(groups)], axis=1
        )

    def active(k):
        return jnp.concatenate(
            [local[k, j * slots : (j + 1) * slots, 256:384] for j in range(groups)], axis=1
        )

    def backward(k):
        for r in range(1, n):
            a_copy(k, r).wait_recv()
        halves[k] = row_side(k, other).astype(jnp.bfloat16)
        h_copy(k).start()

    def give_back(k):
        own = row_side(k, sec)
        h_copy(k).wait_recv()
        whole = (own + got_half[k].astype(jnp.float32)).astype(jnp.bfloat16)

        @pl.when(k == 0)
        def _():
            returned[0] = whole

        @pl.when(k != 0)
        def _():
            back[k - 1] = whole
            r_copy(k).start()


    def nth(turn):
        return jnp.where(turn < 2, turn, n + 1 - turn)

    @pl.loop(0, n + 2)
    def _(turn):
        @pl.when(jnp.logical_and(turn > 0, turn < n))
        def _():
            arrive(nth(turn))

        @pl.when(turn < n)
        def _():
            forward(nth(turn))

        @pl.when(turn == 0)
        def _():
            @pl.loop(0, 2 * width // 256)
            def _(index):
                span = pl.ds(pl.multiple_of(index * 256, 256), 256)
                both_t[:, span] = both_w[span, :].T

        @pl.when(jnp.logical_and(turn > 0, turn <= n))
        def _():
            reduce_local(nth(turn - 1))

        @pl.when(turn > 1)
        def _():
            give_back(nth(turn - 2))

        @pl.when(jnp.logical_and(turn > 0, turn <= n))
        def _():
            backward(nth(turn - 1))

    chunk = 256

    @pl.loop(0, 2 * width // chunk)
    def _(piece):
        per_side = width // chunk
        side = piece // per_side
        low = pl.ds(pl.multiple_of(lax.rem(piece, per_side) * chunk, chunk), chunk)
        span = pl.ds(pl.multiple_of(piece * chunk, chunk), chunk)
        total = contract_rows(
            rows[side, :, low], jnp.concatenate([gate_up(k) for k in range(n)], axis=0)
        ).astype(jnp.bfloat16)
        for j in range(groups):
            gate_g[span, j * 128 : (j + 1) * 128] = total[:, j * 256 : j * 256 + 128]
            up_g[span, j * 128 : (j + 1) * 128] = total[:, j * 256 + 128 : (j + 1) * 256]
        down_g[:, span] = contract_rows(
            jnp.concatenate([active(k) for k in range(n)], axis=0), grads[side, :, low]
        ).astype(jnp.bfloat16)

    stores = [
        pltpu.make_async_copy(gate_g, gate_out, io_sem.at[0]),
        pltpu.make_async_copy(up_g, up_out, io_sem.at[1]),
        pltpu.make_async_copy(down_g, down_out, io_sem.at[2]),
    ]
    for store in stores:
        store.start()

    total = contract_rows(picks[0], returned[0])
    for k in (1, 3, 2):
        r_copy(k).wait_recv()
        total += contract_rows(picks[k], returned[k])
    token_out[...] = total.astype(jnp.bfloat16)

    for k in range(n):
        for copy in s_copies(k):
            copy.wait_send()
        h_copy(k).wait_send()
        for r in range(1, n):
            p_copy(k, r).wait_send()
            a_copy(k, r).wait_send()
        if k > 0:
            for copy in z_copies(k):
                copy.wait_send()
            r_copy(k).wait_send()
    for store in stores:
        store.wait()


def hand_over(count, *refs):
    sources, results, held = refs[:count], refs[count : 2 * count], refs[2 * count : 3 * count]
    load_sem, store_sem = refs[3 * count :]
    loads = [pltpu.make_async_copy(sources[i], held[i], load_sem.at[i]) for i in range(count)]
    stores = [pltpu.make_async_copy(held[i], results[i], store_sem.at[i]) for i in range(count)]
    for load in loads:
        load.start()
    for load, store in zip(loads, stores):
        load.wait()
        store.start()
    for store in stores:
        store.wait()


def on_device_kernel(tokens, out_grad, expert_ids, combine, w_gate, w_up, w_down):
    tok_dev, top_count = expert_ids.shape
    n = lax.axis_size("expert")
    capacity = (tok_dev * top_count * 9 + 8 * n - 1) // (8 * n)
    slots = (capacity + 15) // 16 * 16
    width = tokens.shape[1]
    depth, hidden = w_gate.shape[1:]
    groups = hidden // 128
    share = (groups * slots + 16 * n - 1) // (16 * n) * 16
    bf16 = jnp.bfloat16
    vmem = pl.BlockSpec(memory_space=pltpu.VMEM)
    hbm = pl.BlockSpec(memory_space=pl.ANY)
    dma = pltpu.SemaphoreType.DMA
    results = pl.pallas_call(
        functools.partial(expert_kernel, n, slots),
        out_shape=(
            jax.ShapeDtypeStruct((tok_dev, width), bf16),
            jax.ShapeDtypeStruct((depth, hidden), bf16),
            jax.ShapeDtypeStruct((depth, hidden), bf16),
            jax.ShapeDtypeStruct((hidden, depth), bf16),
        ),
        in_specs=[hbm, hbm, vmem, vmem, hbm, hbm, hbm],
        out_specs=(vmem, hbm, hbm, hbm),
        scratch_shapes=[
            pltpu.VMEM((tok_dev, width), bf16),
            pltpu.VMEM((tok_dev, width), bf16),
            pltpu.VMEM((depth, 2 * hidden), bf16),
            pltpu.VMEM((hidden, depth), bf16),
            pltpu.VMEM((2 * hidden, depth), bf16),
            pltpu.VMEM((depth, hidden), bf16),
            pltpu.VMEM((8, tok_dev), jnp.float32),
            pltpu.VMEM((8, tok_dev), jnp.float32),
            pltpu.VMEM((n, slots, tok_dev), bf16),
            pltpu.VMEM((n - 1, slots, width), bf16),
            pltpu.VMEM((n - 1, slots, width), bf16),
            pltpu.VMEM((2, n * slots, width), bf16),
            pltpu.VMEM((2, n * slots, width), bf16),
            pltpu.VMEM((n, n * share, 384), bf16),
            pltpu.VMEM((n, n - 1, share, 384), bf16),
            pltpu.VMEM((n, n * share, 384), bf16),
            pltpu.VMEM((n, slots, width), bf16),
            pltpu.VMEM((n, slots, width), bf16),
            pltpu.VMEM((n - 1, slots, width), bf16),
            pltpu.VMEM((n, slots, width), bf16),
            pltpu.VMEM((depth, hidden), bf16),
            pltpu.VMEM((depth, hidden), bf16),
            pltpu.VMEM((hidden, depth), bf16),
            dma((3 + 2 * groups,)),
            dma((2, n - 1)),
            dma((2, n - 1)),
            dma((2, n)),
            dma((2, n)),
            dma((n, n - 1)),
            dma((n, n - 1)),
            dma((n, n - 1)),
            dma((n, n - 1)),
            dma((n,)),
            dma((n,)),
            dma((n - 1,)),
            dma((n - 1,)),
        ],
        compiler_params=pltpu.CompilerParams(
            collective_id=0, has_side_effects=True, vmem_limit_bytes=63 * 1024 * 1024
        ),
    )(tokens, out_grad, expert_ids.T, combine.T, w_gate[0], w_up[0], w_down[0])
    token_grad, gate_g, up_g, down_g = pl.pallas_call(
        functools.partial(hand_over, 4),
        out_shape=tuple(jax.ShapeDtypeStruct(result.shape, result.dtype) for result in results),
        in_specs=[hbm] * 4,
        out_specs=(hbm,) * 4,
        scratch_shapes=[pltpu.VMEM(result.shape, bf16) for result in results] + [dma((4,)), dma((4,))],
        compiler_params=pltpu.CompilerParams(vmem_limit_bytes=63 * 1024 * 1024),
    )(*results)
    return (token_grad, gate_g[None], up_g[None], down_g[None])


def fits_kernel(mesh):
    shape = mesh.shape
    return shape["section"] == 2 and shape["expert"] == 4 and shape["tp"] == 4


def solution(mesh):
    return jax.shard_map(
        on_device_kernel if fits_kernel(mesh) else on_device,
        mesh=mesh,
        in_specs=(
            P("expert", ("tp", "section")),
            P("expert", ("tp", "section")),
            P("expert", None),
            P("expert", None),
            P("expert", "tp", "section"),
            P("expert", "tp", "section"),
            P("expert", "section", "tp"),
        ),
        out_specs=(
            P("expert", ("tp", "section")),
            P("expert", "tp", "section"),
            P("expert", "tp", "section"),
            P("expert", "section", "tp"),
        ),
        check_vma=False,
    )
```
